32 devices in a mesh: groups: 2 (over x), tiles: 16 (over z, y, core).
Axes of the slice: x: 2, y: 2, z: 4, core: 2. Of those that a mesh axis runs over, the one named last changes fastest.
Arguments:
- dipoles: bfloat16 [32, 2, 32, 384], P(('groups', 'tiles')), parts along dimension 0, may hold values from -6 to 6
- incident: bfloat16 [32, 2, 32, 384], P(('groups', 'tiles')), parts along dimension 0, may hold values from -6 to 6
- positions: float32 [32, 3, 128], P(('groups', 'tiles')), parts along dimension 0, may hold values from -44 to 44, as said below
- susceptibility: float32 [32, 128], P(('groups', 'tiles')), parts along dimension 0, may hold values from 0.05 to 0.5
- skeleton_sets: int32 [32, 128], P(('groups', 'tiles')), parts along dimension 0, may hold values from 0 to 767, as said below
- near_tiles: int32 [32, 2], P(('groups', 'tiles')), parts along dimension 0, may hold values from 0 to 7, as said below
- compress_fund: bfloat16 [32, 256, 384], P(('groups', 'tiles')), parts along dimension 0, may hold values from -0.21875 to 0.21875
- compress_harm: bfloat16 [32, 256, 384], P(('groups', 'tiles')), parts along dimension 0, may hold values from -0.21875 to 0.21875
Outputs:
- fundamental: float32 [32, 2, 32, 384], P(('groups', 'tiles')), parts along dimension 0
- adjoint_field: float32 [32, 2, 32, 384], P(('groups', 'tiles')), parts along dimension 0
The draws below stay inside these ranges and needn't reach their ends.
There are 2 independent parts, one for each index of `groups`. The reference program is written for one: setup_inputs(seed, part) draws one part's arguments, and reference() takes and returns one part's arrays. A program takes and returns all parts, laid end to end along the dimension named above; each array names one. Nothing has to cross between parts.
Inputs may be any that keep to these rules, and one draw needn't show every extreme that they name: `skeleton_sets`: the 256 entries of tile t (rows 2t and 2t + 1 in order) are distinct. `near_tiles`: each row holds 2 distinct tiles, each differing from the row's own tile s // 2 by 1 or 2 in either direction, cyclically modulo 8. `positions`: distinct points lie at least 1 apart.
All inputs are finite; a program needn't handle non-finite values.
Results may differ from the reference program's by a relative error of at most 0.0051.
Values may be sent and summed in bfloat16 or wider, within the bound.
A program may use at most 128 MiB of HBM per device.

```python
import math
import jax
import jax.numpy as jnp
from jax import lax

POINTS = 256
SKELETONS = 256
ANGLES = 32
NEIGHBORS = 2
HALF_POINTS = 128
HALF_SKELETONS = 128
SLABS = 16
TILES = 8


def draw_positions(key, part):
    key = jax.random.fold_in(key, 11)
    slab_ids = jnp.arange(SLABS)
    tile_ids = (slab_ids // 2).astype(jnp.float32)
    half_ids = (slab_ids % 2).astype(jnp.float32)
    local = jnp.arange(HALF_POINTS)
    tangent_index = (local % 4).astype(jnp.float32)
    radial_index = (local // 4 % 4).astype(jnp.float32)
    vertical_index = (local // 16).astype(jnp.float32)
    vertical_count = HALF_POINTS // 16
    jitter = 0.15 * jax.random.truncated_normal(key, -2.0, 2.0, (SLABS, 3, HALF_POINTS), jnp.float32)
    along = (half_ids[:, None] * 4.0 + tangent_index[None, :] - 3.5) * 2.0 + jitter[:, 0]
    outward = (radial_index[None, :] - 1.5) * 2.0 + jitter[:, 1]
    upward = (vertical_index[None, :] - (vertical_count - 1) / 2.0) * 2.0 + jitter[:, 2]
    angle = 2.0 * math.pi * tile_ids / (SLABS // 2)
    radius = SLABS // 2 * 20.0 / (2.0 * math.pi)
    cosine = jnp.cos(angle)[:, None]
    sine_part = jnp.sin(angle)[:, None]
    coord_x = (radius + outward) * cosine - along * sine_part
    coord_y = (radius + outward) * sine_part + along * cosine
    return jnp.stack([coord_x, coord_y, upward], axis=1).astype(jnp.float32)


def draw_skeleton_sets(key, part):
    key = jax.random.fold_in(key, 23)
    tile_keys = jax.random.split(key, SLABS // 2)

    def choose(tile_key):
        return jax.random.permutation(tile_key, 3 * POINTS)[:SKELETONS]
    chosen = jax.vmap(choose)(tile_keys)
    return chosen.reshape(SLABS, HALF_SKELETONS).astype(jnp.int32)


def draw_near_tiles(key, part):
    key = jax.random.fold_in(key, 37)
    candidates = jnp.array([-2, -1, 1, 2], dtype=jnp.int32)
    slab_keys = jax.random.split(key, SLABS)

    def choose(slab_key):
        return jax.random.permutation(slab_key, 4)[:NEIGHBORS]
    picks = jax.vmap(choose)(slab_keys)
    offsets = candidates[picks]
    own_tiles = (jnp.arange(SLABS, dtype=jnp.int32) // 2)[:, None]
    return ((own_tiles + offsets) % (SLABS // 2)).astype(jnp.int32)


def shard_levels(own_key, shape, cuts, smallest, largest):
    loudness = 1.0
    for dim, shards_of in cuts:
        steps = jax.random.uniform(jax.random.fold_in(jax.random.fold_in(own_key, 6), dim), (shards_of,), jnp.float32, smallest / len(cuts), largest / len(cuts))
        loudness = loudness * jnp.repeat(jnp.exp(steps), shape[dim] // shards_of).reshape((-1,) + (1,) * (len(shape) - 1 - dim))
    return loudness


def bell_draw(rng, dims, deviation, reach, cuts=(), kind=jnp.bfloat16):
    level = shard_levels(rng, dims, cuts, -0.22, 0.18) if cuts else 1.0
    entries = jax.random.normal(rng, dims, jnp.float32) * deviation * level
    return jnp.minimum(jnp.maximum(entries, -reach), reach).astype(kind)


def setup_inputs(seed: int = 0, part: int = 0) -> dict:
    splits = jax.random.split(jax.random.key(seed), 9)
    own_keys = jax.random.split(jax.random.fold_in(splits[8], part), 9)
    dipoles = bell_draw(own_keys[0], (SLABS, 2, ANGLES, 3 * HALF_POINTS), 1.0, 6.0, ((0, 16),))
    incident = bell_draw(own_keys[1], (SLABS, 2, ANGLES, 3 * HALF_POINTS), 1.0, 6.0, ((0, 16),))
    positions = draw_positions(jax.random.fold_in(jax.random.fold_in(splits[8], part), 71), part)
    susceptibility = jnp.clip(jnp.exp(math.log(0.5) - 2.3025851 * jax.random.uniform(own_keys[3], (SLABS, HALF_POINTS), jnp.float32) ** shard_levels(own_keys[3], (SLABS, HALF_POINTS), ((0, 16),), -0.2, 0.2)), 0.05, 0.5)
    skeleton_sets = draw_skeleton_sets(jax.random.fold_in(jax.random.fold_in(splits[8], part), 71), part)
    near_tiles = draw_near_tiles(jax.random.fold_in(jax.random.fold_in(splits[8], part), 71), part)
    compress_fund = bell_draw(own_keys[6], (SLABS, SKELETONS, 3 * HALF_POINTS), (3 * POINTS) ** -0.5, 0.21875, ((0, 16),))
    compress_harm = bell_draw(own_keys[7], (SLABS, SKELETONS, 3 * HALF_POINTS), (3 * POINTS) ** -0.5, 0.21875, ((0, 16),))
    return {"dipoles": dipoles, "incident": incident, "positions": positions, "susceptibility": susceptibility, "skeleton_sets": skeleton_sets, "near_tiles": near_tiles, "compress_fund": compress_fund, "compress_harm": compress_harm}


kernel_scale = 0.5
fund_wave = 0.5
harm_wave = 1.0

def kernel_columns(targets, sources, components, wavenumber, conj_sign):
    separation = targets[:, None, :] - sources[:, :, None]
    squared = lax.optimization_barrier(jnp.sum(separation * separation, axis=0))
    present = squared > 0.0
    distance = jnp.sqrt(jnp.where(present, squared, 1.0))
    direction = separation / distance
    inverse = 1.0 / (wavenumber * distance)
    inverse_sq = inverse * inverse
    projected = jnp.zeros_like(distance)
    for source_axis in range(3):
        projected = projected + jnp.where((components == source_axis)[:, None], direction[source_axis], 0.0)
    amplitude = jnp.where(present, kernel_scale / distance, 0.0)
    cosine = jnp.cos(wavenumber * distance) * amplitude
    sine_part = jnp.sin(wavenumber * distance) * amplitude
    real_rows = []
    imag_rows = []
    for target_axis in range(3):
        matches = (components == target_axis).astype(jnp.float32)[:, None]
        coupling = direction[target_axis] * projected
        alpha_real = (1.0 - inverse_sq) * matches + (3.0 * inverse_sq - 1.0) * coupling
        alpha_imag = inverse * matches - 3.0 * inverse * coupling
        real_rows.append(cosine * alpha_real - sine_part * alpha_imag)
        imag_rows.append(conj_sign * (sine_part * alpha_real + cosine * alpha_imag))
    return jnp.concatenate(real_rows + imag_rows, axis=1).astype(jnp.bfloat16)

def far_sum(accumulated, charges, sources, components, tile_ids, own_tile, nearby, targets, wavenumber, conj_sign, unit_width):
    pieces = charges.shape[1] // unit_width
    grouped = math.gcd(pieces, max(1, 1024 // unit_width))
    block_width = grouped * unit_width

    def advance(number, running):
        offset = number * block_width
        block_charges = lax.dynamic_slice_in_dim(charges, offset, block_width, 1)
        block_sources = lax.dynamic_slice_in_dim(sources, offset, block_width, 1)
        block_parts = lax.dynamic_slice_in_dim(components, offset, block_width, 0)
        block_tiles = lax.dynamic_slice_in_dim(tile_ids, offset, block_width, 0)
        retained = (block_tiles != own_tile) & jnp.all(block_tiles[:, None] != nearby[None, :], axis=1)
        block_charges = block_charges * retained.astype(jnp.bfloat16)[None, :]
        columns = kernel_columns(targets, block_sources, block_parts, wavenumber, conj_sign)
        return running + jnp.dot(block_charges, columns, preferred_element_type=jnp.float32)
    return lax.fori_loop(0, pieces // grouped, advance, accumulated)

def combine_parts(product):
    angles = product.shape[0] // 2
    unknowns = product.shape[1] // 2
    real_part = product[:angles, :unknowns] - product[angles:, unknowns:]
    imag_part = product[:angles, unknowns:] + product[angles:, :unknowns]
    return jnp.stack([real_part, imag_part])

def apply_image(fields, compress, wavenumber, conj_sign, positions, near_tiles, skeleton_points, components, tile_ids):
    flattened = fields.reshape(SLABS, 2 * ANGLES, 3 * HALF_POINTS)
    partial_value = jnp.einsum('srn,skn->srk', flattened.astype(jnp.float32), compress.astype(jnp.float32))
    charges = partial_value.reshape(TILES, 2, 2 * ANGLES, SKELETONS).sum(axis=1)
    charges = charges.transpose(1, 0, 2).reshape(2 * ANGLES, TILES * SKELETONS).astype(jnp.bfloat16)
    triples = jnp.repeat(jnp.arange(3, dtype=jnp.int32), HALF_POINTS)

    def one_slab(my_slab):
        own_tile = my_slab // 2
        nearby = near_tiles[my_slab]
        targets = positions[my_slab]
        zeros_block = jnp.zeros((2 * ANGLES, 6 * HALF_POINTS), jnp.float32)
        far_part = far_sum(zeros_block, charges, skeleton_points, components, tile_ids, own_tile, nearby, targets, wavenumber, conj_sign, SKELETONS)
        halves = jnp.arange(2, dtype=jnp.int32)
        slab_list = jnp.concatenate([2 * own_tile + halves, (2 * nearby[:, None] + halves[None, :]).reshape(-1)]).astype(jnp.int32)

        def add_near(number, running):
            source_slab = slab_list[number]
            block = kernel_columns(targets, jnp.tile(positions[source_slab], (1, 3)), triples, wavenumber, conj_sign)
            return running + jnp.dot(flattened[source_slab], block, preferred_element_type=jnp.float32)
        summed = lax.fori_loop(0, 2 * (NEIGHBORS + 1), add_near, far_part)
        return combine_parts(summed)
    return lax.map(one_slab, jnp.arange(SLABS, dtype=jnp.int32))

def reference(dipoles, incident, positions, susceptibility, skeleton_sets, near_tiles, compress_fund, compress_harm):
    all_points = positions.transpose(1, 0, 2).reshape(3, SLABS * HALF_POINTS)
    skeletons = skeleton_sets.reshape(-1)
    tile_ids = (jnp.arange(TILES * SKELETONS, dtype=jnp.int32) // SKELETONS).astype(jnp.int32)
    point_index = (tile_ids * POINTS + skeletons % POINTS).astype(jnp.int32)
    components = (skeletons // POINTS).astype(jnp.int32)
    skeleton_points = jnp.take(all_points, point_index, axis=1)
    scattered = apply_image(dipoles, compress_fund, fund_wave, 1.0, positions, near_tiles, skeleton_points, components, tile_ids)
    fundamental = incident.astype(jnp.float32) + scattered
    weights = jnp.tile(susceptibility, (1, 3))[:, None, :]
    real_part = fundamental[:, 0]
    imag_part = fundamental[:, 1]
    source = jnp.stack([weights * (real_part * real_part - imag_part * imag_part), weights * 2.0 * real_part * imag_part], axis=1).astype(jnp.bfloat16)
    adjoint_field = apply_image(source, compress_harm, harm_wave, -1.0, positions, near_tiles, skeleton_points, components, tile_ids)
    return (fundamental, adjoint_field)
```

```python
import math

import jax
import jax.numpy as jnp
from jax import lax
from jax.experimental import pallas as pl
from jax.experimental.pallas import tpu as pltpu
from jax.sharding import PartitionSpec as P

POINTS = 256
SKELETONS = 256
ANGLES = 32
HALF = 128
ROWS = 2 * ANGLES
UNKNOWNS = 3 * HALF
CHUNK = 16

fund_wave = 0.5
harm_wave = 1.0

PI_HIGH = 3.140625
PI_LOW = math.pi - 3.140625
COS = (-0.4999993031990062, 0.04166394733655344, -0.0013855657175274386, 2.3189013831140122e-05)
SIN = (-0.16666656730445154, 0.008333010303754999, -0.00019806200404944314, 2.5992746473408684e-06)


def dot_nt(left, right):
    return lax.dot_general(
        left, right, (((1,), (1,)), ((), ())), preferred_element_type=jnp.float32
    )


def pair_terms(target, source, wave, sign):
    diff = [target[a] - source[a] for a in range(3)]
    squared = diff[0] * diff[0] + diff[1] * diff[1] + diff[2] * diff[2]
    present = squared > 0.0
    squared = jnp.where(present, squared, 1.0)
    inverse = lax.rsqrt(squared)
    phase = squared * inverse * wave
    turns = jnp.floor(phase * (1.0 / math.pi) + 0.5)
    rest = (phase - turns * PI_HIGH) - turns * PI_LOW
    half_turns = turns * 0.5
    odd = half_turns - jnp.floor(half_turns)
    amplitude = jnp.where(present, inverse * 0.5, 0.0) * (1.0 - 4.0 * odd)
    rest_sq = rest * rest
    cosine = 1.0 + rest_sq * (
        COS[0] + rest_sq * (COS[1] + rest_sq * (COS[2] + rest_sq * COS[3]))
    )
    sine = rest + rest * rest_sq * (
        SIN[0] + rest_sq * (SIN[1] + rest_sq * (SIN[2] + rest_sq * SIN[3]))
    )
    cosine = cosine * amplitude
    sine = sine * amplitude
    unit = [d * inverse for d in diff]
    z = inverse if wave == 1.0 else inverse * (1.0 / wave)
    z_sq = z * z
    one = 1.0 - z_sq
    three = 3.0 * z_sq - 1.0
    cos_z = cosine * z
    sin_z = sine * z
    same_real = cosine * one - sin_z
    same_imag = sine * one + cos_z
    along_real = cosine * three + 3.0 * sin_z
    along_imag = sine * three - 3.0 * cos_z
    if sign < 0:
        same_imag = -same_imag
        along_imag = -along_imag
    return unit, (same_real, same_imag), (along_real, along_imag)


def body(
    slabs,
    fields_ref,
    incident_ref,
    pos_ref,
    chi_ref,
    skel_ref,
    near_ref,
    vf_ref,
    vh_ref,
    fund_ref,
    adj_ref,
    target_ref,
    pos_all,
    skel_all,
    raw_first,
    raw_second,
    chg_first,
    chg_second,
    part_out,
    part_in,
    near_k,
    far_k,
    acc_ref,
    pos_send,
    pos_recv,
    skel_send,
    skel_recv,
    raw_send,
    raw_recv,
    chg_send,
    chg_recv,
    part_send,
    part_recv,
):
    tiles = slabs // 2
    raw_all = (raw_first, raw_second)
    chg_all = (chg_first, chg_second)
    group = lax.axis_index("groups")
    me = lax.axis_index("tiles")
    own_tile = lax.div(me, 2)
    my_half = lax.rem(me, 2)
    partner = own_tile * 2 + (1 - my_half)

    def peer(step):
        return lax.rem(me + step, slabs)

    def wrap_tile(t):
        return lax.rem(t + tiles, tiles)

    near_peers = [(partner, 4 + (1 - my_half), 4 + my_half)]
    for d in (-1, 1, -2, 2):
        for h in range(2):
            slab = wrap_tile(own_tile + d) * 2 + h
            near_peers.append((slab, (d + 2) * 2 + h, (2 - d) * 2 + my_half))

    barrier = pltpu.get_barrier_semaphore()

    def greet(step, carry):
        pl.semaphore_signal(
            barrier, inc=1, device_id=(group, peer(step)), device_id_type=pl.DeviceIdType.MESH
        )
        return carry

    lax.fori_loop(1, slabs, greet, 0)

    def copy(src, dst, send, recv, slab):
        return pltpu.make_async_remote_copy(
            src_ref=src,
            dst_ref=dst,
            send_sem=send,
            recv_sem=recv,
            device_id=(group, slab),
            device_id_type=pl.DeviceIdType.MESH,
        )

    def partial(phase, fields, v_ref):
        part_out[phase, 0] = dot_nt(fields, v_ref[0:HALF, :])
        part_out[phase, 1] = dot_nt(fields, v_ref[HALF:, :])

    def part_copy(phase):
        return copy(
            part_out.at[phase, 1 - my_half],
            part_in.at[phase],
            part_send.at[phase],
            part_recv.at[phase],
            partner,
        )

    own_slot = 4 + my_half

    def raw_copy(phase, number):
        slab, here, there = near_peers[number]
        return copy(
            raw_all[phase].at[own_slot],
            raw_all[phase].at[there],
            raw_send.at[phase, number],
            raw_recv.at[phase, there],
            slab,
        )

    def raw_arrival(phase, number):
        slab, here, there = near_peers[number]
        return copy(
            raw_all[phase].at[own_slot],
            raw_all[phase].at[here],
            raw_send.at[phase, number],
            raw_recv.at[phase, here],
            slab,
        )

    def pos_copy(number):
        slab, here, there = near_peers[number]
        return copy(
            pos_all.at[own_slot],
            pos_all.at[there],
            pos_send.at[number],
            pos_recv.at[there],
            slab,
        )

    def pos_arrival(number):
        slab, here, there = near_peers[number]
        return copy(
            pos_all.at[own_slot],
            pos_all.at[here],
            pos_send.at[number],
            pos_recv.at[here],
            slab,
        )

    def skel_copy(step, slot):
        return copy(
            skel_all.at[me], skel_all.at[slot], skel_send.at[step], skel_recv.at[slot], peer(step)
        )

    def chg_copy(phase, step, slot):
        return copy(
            chg_all[phase].at[me],
            chg_all[phase].at[slot],
            chg_send.at[phase, step],
            chg_recv.at[phase, slot],
            peer(step),
        )

    def each_peer(act):
        def go(step, carry):
            act(step)
            return carry

        lax.fori_loop(1, slabs, go, 0)

    def send_charges(phase):
        part_copy(phase).wait_recv()
        summed = part_out[phase, my_half] + part_in[phase]
        chg_all[phase][me] = summed.astype(jnp.bfloat16)
        each_peer(lambda step: chg_copy(phase, step, me).start())

    first, second = near_ref[0, 0], near_ref[0, 1]

    def near_slot(t):
        d = t - own_tile + 2
        d = jnp.where(d < 0, d + tiles, d)
        d = jnp.where(d >= tiles, d - tiles, d)
        return jnp.minimum(jnp.maximum(d, 0), 4)

    def near_place(place):
        return near_slot(
            jnp.where(place == 0, own_tile, jnp.where(place == 1, first, second))
        )

    low = jnp.minimum(own_tile, jnp.minimum(first, second))
    high = jnp.maximum(own_tile, jnp.maximum(first, second))
    middle = own_tile + first + second - low - high

    def far_tile(number):
        t = jnp.where(number >= low, number + 1, number)
        t = jnp.where(t >= middle, t + 1, t)
        return jnp.minimum(jnp.where(t >= high, t + 1, t), tiles - 1)

    def near_eval(place, half, wave, sign, own):
        block = pos_all[4 + half if own else near_place(place) * 2 + half]
        source = [block[a : a + 1, :] for a in range(3)]
        for chunk in range(HALF // CHUNK):
            rows = slice(chunk * CHUNK, (chunk + 1) * CHUNK)
            target = [target_ref[a, rows, :] for a in range(3)]
            unit, same, along = pair_terms(target, source, wave, sign)
            for part in range(2):
                scaled = [along[part] * unit[a] for a in range(3)]
                for a in range(3):
                    for b in range(a, 3):
                        value = scaled[a] * unit[b]
                        if a == b:
                            value = value + same[part]
                        value = value.astype(jnp.bfloat16)
                        for p, q in [(a, b), (b, a)][: 1 + (a != b)]:
                            start = part * UNKNOWNS + p * HALF + chunk * CHUNK
                            near_k[
                                place * 2 + half, start : start + CHUNK, q * HALF : (q + 1) * HALF
                            ] = value

    def far_eval(number, half, wave, sign):
        block = skel_all[far_tile(number) * 2 + half]
        source = [block[a : a + 1, :] for a in range(3)]
        which = [block[3 + a : 4 + a, :] for a in range(3)]
        for chunk in range(HALF // CHUNK):
            rows = slice(chunk * CHUNK, (chunk + 1) * CHUNK)
            target = [target_ref[a, rows, :] for a in range(3)]
            unit, same, along = pair_terms(target, source, wave, sign)
            projected = unit[0] * which[0] + unit[1] * which[1] + unit[2] * which[2]
            for part in range(2):
                scaled = along[part] * projected
                for a in range(3):
                    value = scaled * unit[a] + same[part] * which[a]
                    start = part * UNKNOWNS + a * HALF + chunk * CHUNK
                    far_k[number * 2 + half, start : start + CHUNK, :] = value.astype(jnp.bfloat16)

    def eval_near_from(start, stop, wave, sign):
        def go(index, carry):
            near_eval(lax.div(index, 2), lax.rem(index, 2), wave, sign, start == 0)
            return carry

        lax.fori_loop(2 * start, 2 * stop, go, 0)

    def eval_far(wave, sign):
        def go(index, carry):
            far_eval(lax.div(index, 2), lax.rem(index, 2), wave, sign)
            return carry

        lax.fori_loop(0, 2 * (tiles - 3), go, 0)

    def multiply_near(phase):
        def go(place, carry):
            slot = near_place(place) * 2
            acc_ref[...] += dot_nt(raw_all[phase][slot], near_k[place * 2]) + dot_nt(
                raw_all[phase][slot + 1], near_k[place * 2 + 1]
            )
            return carry

        lax.fori_loop(0, 3, go, 0)

    def multiply_far(phase):
        def go(number, carry):
            slot = far_tile(number) * 2
            charges = jnp.concatenate([chg_all[phase][slot], chg_all[phase][slot + 1]], axis=1)
            columns = jnp.concatenate([far_k[number * 2], far_k[number * 2 + 1]], axis=1)
            acc_ref[...] += dot_nt(charges, columns)
            return carry

        lax.fori_loop(0, tiles - 3, go, 0)

    def combined():
        real = acc_ref[:ANGLES, :UNKNOWNS] - acc_ref[ANGLES:, UNKNOWNS:]
        imag = acc_ref[:ANGLES, UNKNOWNS:] + acc_ref[ANGLES:, :UNKNOWNS]
        return real, imag

    raw_all[0][own_slot] = fields_ref[...]
    pos_all[own_slot, 0:3, :] = pos_ref[...]
    pos_all[own_slot, 3:8, :] = jnp.zeros((5, HALF), jnp.float32)
    partial(0, fields_ref[...], vf_ref)
    for a in range(3):
        target_ref[a] = jnp.broadcast_to(pos_ref[a : a + 1, :], (HALF, HALF)).T
    pl.semaphore_wait(barrier, slabs - 1)
    for number in range(9):
        pos_copy(number).start()
    part_copy(0).start()
    for number in range(9):
        raw_copy(0, number).start()
    acc_ref[...] = jnp.zeros_like(acc_ref)

    pos_arrival(0).wait_recv()
    skeleton = skel_ref[...]
    component = jnp.where(skeleton >= 2 * POINTS, 2, jnp.where(skeleton >= POINTS, 1, 0))
    point = skeleton - component * POINTS
    lines = lax.broadcasted_iota(jnp.int32, (HALF, HALF), 0)
    masks = [lines + HALF * h == point for h in range(2)]
    other = pos_all[4 + (1 - my_half)]
    packet = []
    for a in range(3):
        own_column = target_ref[a]
        other_column = jnp.broadcast_to(other[a : a + 1, :], (HALF, HALF)).T
        columns = [
            jnp.where(my_half == 0, own_column, other_column),
            jnp.where(my_half == 0, other_column, own_column),
        ]
        picked = jnp.where(masks[0], columns[0], jnp.where(masks[1], columns[1], 0.0))
        packet.append(jnp.sum(picked, axis=0, keepdims=True))
    for a in range(3):
        packet.append((component == a).astype(jnp.float32))
    packet.append(jnp.zeros((2, HALF), jnp.float32))
    skel_all[me] = jnp.concatenate(packet, axis=0)
    each_peer(lambda step: skel_copy(step, me).start())
    send_charges(0)

    eval_near_from(0, 1, fund_wave, 1.0)
    for number in range(1, 9):
        pos_arrival(number).wait_recv()
    eval_near_from(1, 3, fund_wave, 1.0)
    each_peer(lambda step: skel_copy(step, peer(step)).wait_recv())
    eval_far(fund_wave, 1.0)
    for number in range(9):
        raw_arrival(0, number).wait_recv()
    multiply_near(0)
    each_peer(lambda step: chg_copy(0, step, peer(step)).wait_recv())
    multiply_far(0)

    real, imag = combined()
    real = incident_ref[:ANGLES, :].astype(jnp.float32) + real
    imag = incident_ref[ANGLES:, :].astype(jnp.float32) + imag
    fund_ref[:ANGLES, :] = real
    fund_ref[ANGLES:, :] = imag
    weights = jnp.concatenate([chi_ref[...]] * 3, axis=1)
    source = jnp.concatenate(
        [weights * (real * real - imag * imag), weights * 2.0 * real * imag], axis=0
    ).astype(jnp.bfloat16)

    raw_all[1][own_slot] = source
    partial(1, source, vh_ref)
    part_copy(1).start()
    for number in range(9):
        raw_copy(1, number).start()
    acc_ref[...] = jnp.zeros_like(acc_ref)
    eval_near_from(0, 1, harm_wave, -1.0)
    send_charges(1)
    eval_near_from(1, 3, harm_wave, -1.0)
    eval_far(harm_wave, -1.0)
    for number in range(9):
        raw_arrival(1, number).wait_recv()
    multiply_near(1)
    each_peer(lambda step: chg_copy(1, step, peer(step)).wait_recv())
    multiply_far(1)
    real, imag = combined()
    adj_ref[:ANGLES, :] = real
    adj_ref[ANGLES:, :] = imag

    for number in range(9):
        pos_copy(number).wait_send()
    for phase in range(2):
        part_copy(phase).wait_send()
        for number in range(9):
            raw_copy(phase, number).wait_send()
        each_peer(lambda step: chg_copy(phase, step, me).wait_send())
    each_peer(lambda step: skel_copy(step, me).wait_send())


def solution(mesh):
    slabs = mesh.shape["tiles"]
    tiles = slabs // 2
    bf16, f32 = jnp.bfloat16, jnp.float32
    dma = pltpu.SemaphoreType.DMA
    vmem = pl.BlockSpec(memory_space=pltpu.VMEM)

    def on_device(dipoles, incident, positions, chi, skeletons, near, vf, vh):
        fields = dipoles.reshape(ROWS, UNKNOWNS)
        out = jax.ShapeDtypeStruct((ROWS, UNKNOWNS), f32)
        fund, adj = pl.pallas_call(
            lambda *refs: body(slabs, *refs),
            out_shape=(out, out),
            in_specs=[vmem] * 5 + [pl.BlockSpec(memory_space=pltpu.SMEM)] + [vmem] * 2,
            out_specs=(vmem, vmem),
            scratch_shapes=[
                pltpu.VMEM((3, HALF, HALF), f32),
                pltpu.VMEM((10, 8, HALF), f32),
                pltpu.VMEM((slabs, 8, HALF), f32),
                pltpu.VMEM((10, ROWS, UNKNOWNS), bf16),
                pltpu.VMEM((10, ROWS, UNKNOWNS), bf16),
                pltpu.VMEM((slabs, ROWS, HALF), bf16),
                pltpu.VMEM((slabs, ROWS, HALF), bf16),
                pltpu.VMEM((2, 2, ROWS, HALF), f32),
                pltpu.VMEM((2, ROWS, HALF), f32),
                pltpu.VMEM((6, 2 * UNKNOWNS, UNKNOWNS), bf16),
                pltpu.VMEM((2 * (tiles - 3), 2 * UNKNOWNS, HALF), bf16),
                pltpu.VMEM((ROWS, 2 * UNKNOWNS), f32),
                dma((9,)),
                dma((10,)),
                dma((slabs,)),
                dma((slabs,)),
                dma((2, 9)),
                dma((2, 10)),
                dma((2, slabs)),
                dma((2, slabs)),
                dma((2,)),
                dma((2,)),
            ],
            compiler_params=pltpu.CompilerParams(
                collective_id=0, has_side_effects=True, vmem_limit_bytes=50 * 2**20
            ),
            name="images",
        )(
            fields,
            incident.reshape(ROWS, UNKNOWNS),
            positions[0],
            chi,
            skeletons,
            near,
            vf[0],
            vh[0],
        )
        shape = (1, 2, ANGLES, UNKNOWNS)
        return fund.reshape(shape), adj.reshape(shape)

    row = ("groups", "tiles")
    in_specs = (
        P(row, None, None, None),
        P(row, None, None, None),
        P(row, None, None),
        P(row, None),
        P(row, None),
        P(row, None),
        P(row, None, None),
        P(row, None, None),
    )
    out_specs = (P(row, None, None, None), P(row, None, None, None))
    return jax.shard_map(
        on_device, mesh=mesh, in_specs=in_specs, out_specs=out_specs, check_vma=False
    )
```

```python
import math

import jax
import jax.numpy as jnp
from jax import lax
from jax.experimental import pallas as pl
from jax.experimental.pallas import tpu as pltpu
from jax.sharding import PartitionSpec as P

POINTS = 256
SKELETONS = 256
ANGLES = 32
HALF = 128
ROWS = 2 * ANGLES
UNKNOWNS = 3 * HALF
CHUNK = 16

fund_wave = 0.5
harm_wave = 1.0

PI_HIGH = 3.140625
PI_LOW = math.pi - 3.140625
COS = (-0.4999993031990062, 0.04166394733655344, -0.0013855657175274386, 2.3189013831140122e-05)
SIN = (-0.16666656730445154, 0.008333010303754999, -0.00019806200404944314, 2.5992746473408684e-06)


def dot_nt(left, right):
    return lax.dot_general(
        left, right, (((1,), (1,)), ((), ())), preferred_element_type=jnp.float32
    )


def pair_terms(target, source, wave, sign):
    diff = [target[a] - source[a] for a in range(3)]
    squared = diff[0] * diff[0] + diff[1] * diff[1] + diff[2] * diff[2]
    present = squared > 0.0
    squared = jnp.where(present, squared, 1.0)
    inverse = lax.rsqrt(squared)
    phase = squared * inverse * wave
    turns = jnp.floor(phase * (1.0 / math.pi) + 0.5)
    rest = (phase - turns * PI_HIGH) - turns * PI_LOW
    half_turns = turns * 0.5
    odd = half_turns - jnp.floor(half_turns)
    amplitude = jnp.where(present, inverse * 0.5, 0.0) * (1.0 - 4.0 * odd)
    rest_sq = rest * rest
    cosine = 1.0 + rest_sq * (
        COS[0] + rest_sq * (COS[1] + rest_sq * (COS[2] + rest_sq * COS[3]))
    )
    sine = rest + rest * rest_sq * (
        SIN[0] + rest_sq * (SIN[1] + rest_sq * (SIN[2] + rest_sq * SIN[3]))
    )
    cosine = cosine * amplitude
    sine = sine * amplitude
    unit = [d * inverse for d in diff]
    z = inverse if wave == 1.0 else inverse * (1.0 / wave)
    z_sq = z * z
    one = 1.0 - z_sq
    three = 3.0 * z_sq - 1.0
    cos_z = cosine * z
    sin_z = sine * z
    same_real = cosine * one - sin_z
    same_imag = sine * one + cos_z
    along_real = cosine * three + 3.0 * sin_z
    along_imag = sine * three - 3.0 * cos_z
    if sign < 0:
        same_imag = -same_imag
        along_imag = -along_imag
    return unit, (same_real, same_imag), (along_real, along_imag)


def body(
    slabs,
    fields_in,
    incident_in,
    pos_in,
    chi_in,
    skel_in,
    near_ref,
    vf_in,
    vh_in,
    fund_ref,
    adj_ref,
    incident_ref,
    chi_ref,
    skel_ref,
    vf_ref,
    vh_ref,
    target_ref,
    pos_all,
    skel_all,
    raw_first,
    raw_second,
    chg_first,
    chg_second,
    part_out,
    part_in,
    near_k,
    far_k,
    acc_ref,
    pos_send,
    pos_recv,
    skel_send,
    skel_recv,
    raw_send,
    raw_recv,
    chg_send,
    chg_recv,
    part_send,
    part_recv,
    load_sem,
):
    tiles = slabs // 2
    raw_all = (raw_first, raw_second)
    chg_all = (chg_first, chg_second)
    group = lax.axis_index("groups")
    me = lax.axis_index("tiles")
    own_tile = lax.div(me, 2)
    my_half = lax.rem(me, 2)
    partner = own_tile * 2 + (1 - my_half)

    def peer(step):
        return lax.rem(me + 2 * step, slabs)

    def wrap_tile(t):
        return lax.rem(t + tiles, tiles)

    near_peers = [(d, wrap_tile(own_tile + d) * 2 + my_half) for d in (-1, 1, -2, 2)]
    own_slot = 4 + my_half

    def slot_of(d, half):
        return (d + 2) * 2 + half

    barrier = pltpu.get_barrier_semaphore()

    def greet(step, carry):
        pl.semaphore_signal(
            barrier, inc=1, device_id=(group, peer(step)), device_id_type=pl.DeviceIdType.MESH
        )
        return carry

    pl.semaphore_signal(
        barrier, inc=1, device_id=(group, partner), device_id_type=pl.DeviceIdType.MESH
    )
    lax.fori_loop(1, tiles, greet, 0)

    def copy(src, dst, send, recv, slab):
        return pltpu.make_async_remote_copy(
            src_ref=src,
            dst_ref=dst,
            send_sem=send,
            recv_sem=recv,
            device_id=(group, slab),
            device_id_type=pl.DeviceIdType.MESH,
        )

    def partial(phase, fields, v_ref):
        part_out[phase, 0] = dot_nt(fields, v_ref[0:HALF, :])
        part_out[phase, 1] = dot_nt(fields, v_ref[HALF:, :])

    def part_copy(phase):
        return copy(
            part_out.at[phase, 1 - my_half],
            part_in.at[phase],
            part_send.at[phase],
            part_recv.at[phase],
            partner,
        )

    def near_sends(buffer, send, recv):
        copy(buffer.at[own_slot], buffer.at[own_slot], send.at[0], recv.at[own_slot], partner).start()
        for number, (d, slab) in enumerate(near_peers):
            slot = slot_of(-d, my_half)
            copy(buffer.at[own_slot], buffer.at[slot], send.at[1 + number], recv.at[slot], slab).start()

    def near_wait(buffer, send, recv, slot):
        copy(buffer.at[own_slot], buffer.at[slot], send.at[0], recv.at[slot], partner).wait_recv()

    def near_forward(buffer, send, recv):
        for number, (d, slab) in enumerate(near_peers):
            slot = slot_of(d, my_half)
            near_wait(buffer, send, recv, slot)
            copy(buffer.at[slot], buffer.at[slot], send.at[5 + number], recv.at[slot], partner).start()

    def near_arrive(buffer, send, recv, with_partner):
        if with_partner:
            near_wait(buffer, send, recv, 5 - my_half)
        for d, slab in near_peers:
            near_wait(buffer, send, recv, slot_of(d, 1 - my_half))

    def near_sent(buffer, send, recv):
        for number in range(9):
            copy(
                buffer.at[own_slot], buffer.at[own_slot], send.at[number], recv.at[own_slot], partner
            ).wait_send()

    def loop(act):
        def go(step, carry):
            act(step)
            return carry

        lax.fori_loop(1, tiles, go, 0)

    def far_sends(buffer, send, recv):
        copy(buffer.at[me], buffer.at[me], send.at[0], recv.at[me], partner).start()
        loop(
            lambda step: copy(
                buffer.at[me], buffer.at[me], send.at[step], recv.at[me], peer(step)
            ).start()
        )

    def far_wait(buffer, send, recv, slab):
        copy(buffer.at[me], buffer.at[slab], send.at[0], recv.at[slab], partner).wait_recv()

    def far_forward(buffer, send, recv):
        def act(step):
            slab = peer(step)
            far_wait(buffer, send, recv, slab)
            copy(
                buffer.at[slab], buffer.at[slab], send.at[tiles - 1 + step], recv.at[slab], partner
            ).start()

        loop(act)

    def far_arrive(buffer, send, recv):
        far_wait(buffer, send, recv, partner)
        loop(lambda step: far_wait(buffer, send, recv, lax.rem(partner + 2 * step, slabs)))

    def far_sent(buffer, send, recv):
        def go(number, carry):
            copy(buffer.at[me], buffer.at[me], send.at[number], recv.at[me], partner).wait_send()
            return carry

        lax.fori_loop(0, slabs - 1, go, 0)

    pos_set = (pos_all, pos_send, pos_recv)
    skel_set = (skel_all, skel_send, skel_recv)
    raw_set = [(raw_all[p], raw_send.at[p], raw_recv.at[p]) for p in range(2)]
    chg_set = [(chg_all[p], chg_send.at[p], chg_recv.at[p]) for p in range(2)]

    def send_charges(phase):
        part_copy(phase).wait_recv()
        summed = part_out[phase, my_half] + part_in[phase]
        chg_all[phase][me] = summed.astype(jnp.bfloat16)
        far_sends(*chg_set[phase])

    first, second = near_ref[0, 0], near_ref[0, 1]

    def near_slot(t):
        d = t - own_tile + 2
        d = jnp.where(d < 0, d + tiles, d)
        d = jnp.where(d >= tiles, d - tiles, d)
        return jnp.minimum(jnp.maximum(d, 0), 4)

    def near_place(place):
        return near_slot(
            jnp.where(place == 0, own_tile, jnp.where(place == 1, first, second))
        )

    low = jnp.minimum(own_tile, jnp.minimum(first, second))
    high = jnp.maximum(own_tile, jnp.maximum(first, second))
    middle = own_tile + first + second - low - high

    def far_tile(number):
        t = jnp.where(number >= low, number + 1, number)
        t = jnp.where(t >= middle, t + 1, t)
        return jnp.minimum(jnp.where(t >= high, t + 1, t), tiles - 1)

    def near_eval(place, half, wave, sign, own):
        block = pos_all[4 + half if own else near_place(place) * 2 + half]
        source = [block[a : a + 1, :] for a in range(3)]
        for chunk in range(HALF // CHUNK):
            rows = slice(chunk * CHUNK, (chunk + 1) * CHUNK)
            target = [target_ref[a, rows, :] for a in range(3)]
            unit, same, along = pair_terms(target, source, wave, sign)
            for part in range(2):
                scaled = [along[part] * unit[a] for a in range(3)]
                for a in range(3):
                    for b in range(a, 3):
                        value = scaled[a] * unit[b]
                        if a == b:
                            value = value + same[part]
                        value = value.astype(jnp.bfloat16)
                        for p, q in [(a, b), (b, a)][: 1 + (a != b)]:
                            start = part * UNKNOWNS + p * HALF + chunk * CHUNK
                            near_k[
                                place * 2 + half, start : start + CHUNK, q * HALF : (q + 1) * HALF
                            ] = value

    def far_eval(number, half, wave, sign):
        block = skel_all[far_tile(number) * 2 + half]
        source = [block[a : a + 1, :] for a in range(3)]
        which = [block[3 + a : 4 + a, :] for a in range(3)]
        for chunk in range(HALF // CHUNK):
            rows = slice(chunk * CHUNK, (chunk + 1) * CHUNK)
            target = [target_ref[a, rows, :] for a in range(3)]
            unit, same, along = pair_terms(target, source, wave, sign)
            projected = unit[0] * which[0] + unit[1] * which[1] + unit[2] * which[2]
            for part in range(2):
                scaled = along[part] * projected
                for a in range(3):
                    value = scaled * unit[a] + same[part] * which[a]
                    start = part * UNKNOWNS + a * HALF + chunk * CHUNK
                    far_k[number * 2 + half, start : start + CHUNK, :] = value.astype(jnp.bfloat16)

    def eval_near_from(start, stop, wave, sign):
        def go(index, carry):
            near_eval(lax.div(index, 2), lax.rem(index, 2), wave, sign, start == 0)
            return carry

        lax.fori_loop(2 * start, 2 * stop, go, 0)

    def eval_far(start, stop, wave, sign):
        def go(index, carry):
            far_eval(lax.div(index, 2), lax.rem(index, 2), wave, sign)
            return carry

        lax.fori_loop(2 * start, 2 * stop, go, 0)

    def multiply_near(phase):
        def go(place, carry):
            slot = near_place(place) * 2
            acc_ref[...] += dot_nt(raw_all[phase][slot], near_k[place * 2]) + dot_nt(
                raw_all[phase][slot + 1], near_k[place * 2 + 1]
            )
            return carry

        lax.fori_loop(0, 3, go, 0)

    def multiply_far(phase):
        def go(number, carry):
            slot = far_tile(number) * 2
            charges = jnp.concatenate([chg_all[phase][slot], chg_all[phase][slot + 1]], axis=1)
            columns = jnp.concatenate([far_k[number * 2], far_k[number * 2 + 1]], axis=1)
            acc_ref[...] += dot_nt(charges, columns)
            return carry

        lax.fori_loop(0, tiles - 3, go, 0)

    def combined():
        real = acc_ref[:ANGLES, :UNKNOWNS] - acc_ref[ANGLES:, UNKNOWNS:]
        imag = acc_ref[:ANGLES, UNKNOWNS:] + acc_ref[ANGLES:, :UNKNOWNS]
        return real, imag

    loads = [
        pltpu.make_async_copy(src, dst, load_sem.at[number])
        for number, (src, dst) in enumerate(
            [
                (pos_in, pos_all.at[own_slot]),
                (fields_in, raw_all[0].at[own_slot]),
                (vf_in, vf_ref),
                (skel_in, skel_ref),
                (chi_in, chi_ref),
                (incident_in, incident_ref),
                (vh_in, vh_ref),
            ]
        )
    ]
    for load in loads:
        load.start()
    acc_ref[...] = jnp.zeros_like(acc_ref)
    loads[0].wait()
    for a in range(3):
        target_ref[a] = jnp.broadcast_to(pos_all[own_slot, a : a + 1, :], (HALF, HALF)).T
    loads[1].wait()
    loads[2].wait()
    partial(0, raw_all[0][own_slot], vf_ref)
    pl.semaphore_wait(barrier, tiles)
    near_sends(*pos_set)
    part_copy(0).start()
    near_sends(*raw_set[0])
    loads[3].wait()

    near_wait(*pos_set, 5 - my_half)
    skeleton = skel_ref[...]
    component = jnp.where(skeleton >= 2 * POINTS, 2, jnp.where(skeleton >= POINTS, 1, 0))
    point = skeleton - component * POINTS
    lines = lax.broadcasted_iota(jnp.int32, (HALF, HALF), 0)
    masks = [lines + HALF * h == point for h in range(2)]
    other = pos_all[4 + (1 - my_half)]
    packet = []
    for a in range(3):
        own_column = target_ref[a]
        other_column = jnp.broadcast_to(other[a : a + 1, :], (HALF, HALF)).T
        columns = [
            jnp.where(my_half == 0, own_column, other_column),
            jnp.where(my_half == 0, other_column, own_column),
        ]
        picked = jnp.where(masks[0], columns[0], jnp.where(masks[1], columns[1], 0.0))
        packet.append(jnp.sum(picked, axis=0, keepdims=True))
    for a in range(3):
        packet.append((component == a).astype(jnp.float32))
    packet.append(jnp.zeros((2, HALF), jnp.float32))
    skel_all[me] = jnp.concatenate(packet, axis=0)
    far_sends(*skel_set)
    send_charges(0)

    near_forward(*pos_set)
    eval_near_from(0, 1, fund_wave, 1.0)
    far_forward(*skel_set)
    near_arrive(*pos_set, False)
    eval_near_from(1, 3, fund_wave, 1.0)
    near_forward(*raw_set[0])
    far_arrive(*skel_set)
    split = (tiles - 3) // 2
    eval_far(0, split, fund_wave, 1.0)
    far_forward(*chg_set[0])
    eval_far(split, tiles - 3, fund_wave, 1.0)
    near_arrive(*raw_set[0], True)
    multiply_near(0)
    far_arrive(*chg_set[0])
    multiply_far(0)

    loads[4].wait()
    loads[5].wait()
    loads[6].wait()
    real, imag = combined()
    real = incident_ref[:ANGLES, :].astype(jnp.float32) + real
    imag = incident_ref[ANGLES:, :].astype(jnp.float32) + imag
    fund_ref[:ANGLES, :] = real
    fund_ref[ANGLES:, :] = imag
    weights = jnp.concatenate([chi_ref[...]] * 3, axis=1)
    source = jnp.concatenate(
        [weights * (real * real - imag * imag), weights * 2.0 * real * imag], axis=0
    ).astype(jnp.bfloat16)

    raw_all[1][own_slot] = source
    partial(1, source, vh_ref)
    part_copy(1).start()
    near_sends(*raw_set[1])
    acc_ref[...] = jnp.zeros_like(acc_ref)
    eval_near_from(0, 1, harm_wave, -1.0)
    send_charges(1)
    eval_near_from(1, 3, harm_wave, -1.0)
    near_forward(*raw_set[1])
    eval_far(0, split, harm_wave, -1.0)
    far_forward(*chg_set[1])
    eval_far(split, tiles - 3, harm_wave, -1.0)
    near_arrive(*raw_set[1], True)
    multiply_near(1)
    far_arrive(*chg_set[1])
    multiply_far(1)
    real, imag = combined()
    adj_ref[:ANGLES, :] = real
    adj_ref[ANGLES:, :] = imag

    near_sent(*pos_set)
    far_sent(*skel_set)
    for phase in range(2):
        part_copy(phase).wait_send()
        near_sent(*raw_set[phase])
        far_sent(*chg_set[phase])


def solution(mesh):
    slabs = mesh.shape["tiles"]
    tiles = slabs // 2
    bf16, f32 = jnp.bfloat16, jnp.float32
    dma = pltpu.SemaphoreType.DMA
    hbm = pl.BlockSpec(memory_space=pltpu.HBM)
    vmem = pl.BlockSpec(memory_space=pltpu.VMEM)

    def on_device(dipoles, incident, positions, chi, skeletons, near, vf, vh):
        fields = dipoles.reshape(ROWS, UNKNOWNS)
        out = jax.ShapeDtypeStruct((ROWS, UNKNOWNS), f32)
        fund, adj = pl.pallas_call(
            lambda *refs: body(slabs, *refs),
            out_shape=(out, out),
            in_specs=[hbm] * 5 + [pl.BlockSpec(memory_space=pltpu.SMEM)] + [hbm] * 2,
            out_specs=(vmem, vmem),
            scratch_shapes=[
                pltpu.VMEM((ROWS, UNKNOWNS), bf16),
                pltpu.VMEM((1, HALF), f32),
                pltpu.VMEM((1, HALF), jnp.int32),
                pltpu.VMEM((SKELETONS, UNKNOWNS), bf16),
                pltpu.VMEM((SKELETONS, UNKNOWNS), bf16),
                pltpu.VMEM((3, HALF, HALF), f32),
                pltpu.VMEM((10, 3, HALF), f32),
                pltpu.VMEM((slabs, 8, HALF), f32),
                pltpu.VMEM((10, ROWS, UNKNOWNS), bf16),
                pltpu.VMEM((10, ROWS, UNKNOWNS), bf16),
                pltpu.VMEM((slabs, ROWS, HALF), bf16),
                pltpu.VMEM((slabs, ROWS, HALF), bf16),
                pltpu.VMEM((2, 2, ROWS, HALF), f32),
                pltpu.VMEM((2, ROWS, HALF), f32),
                pltpu.VMEM((6, 2 * UNKNOWNS, UNKNOWNS), bf16),
                pltpu.VMEM((2 * (tiles - 3), 2 * UNKNOWNS, HALF), bf16),
                pltpu.VMEM((ROWS, 2 * UNKNOWNS), f32),
                dma((9,)),
                dma((10,)),
                dma((slabs,)),
                dma((slabs,)),
                dma((2, 9)),
                dma((2, 10)),
                dma((2, slabs)),
                dma((2, slabs)),
                dma((2,)),
                dma((2,)),
                dma((7,)),
            ],
            compiler_params=pltpu.CompilerParams(
                collective_id=0, has_side_effects=True, vmem_limit_bytes=50 * 2**20
            ),
            name="images",
        )(
            fields,
            incident.reshape(ROWS, UNKNOWNS),
            positions[0],
            chi,
            skeletons,
            near,
            vf[0],
            vh[0],
        )
        shape = (1, 2, ANGLES, UNKNOWNS)
        return fund.reshape(shape), adj.reshape(shape)

    row = ("groups", "tiles")
    in_specs = (
        P(row, None, None, None),
        P(row, None, None, None),
        P(row, None, None),
        P(row, None),
        P(row, None),
        P(row, None),
        P(row, None, None),
        P(row, None, None),
    )
    out_specs = (P(row, None, None, None), P(row, None, None, None))
    return jax.shard_map(
        on_device, mesh=mesh, in_specs=in_specs, out_specs=out_specs, check_vma=False
    )
```

```python
import math

import jax
import jax.numpy as jnp
from jax import lax
from jax.experimental import pallas as pl
from jax.experimental.pallas import tpu as pltpu
from jax.sharding import PartitionSpec as P

POINTS = 256
SKELETONS = 256
ANGLES = 32
HALF = 128
ROWS = 2 * ANGLES
UNKNOWNS = 3 * HALF
CHUNK = 16
VMEM = 64 * 2**20 - 64 * 1024

fund_wave = 0.5
harm_wave = 1.0

PI_HIGH = 3.140625
PI_LOW = math.pi - 3.140625
COS = (-0.4999993031990062, 0.04166394733655344, -0.0013855657175274386, 2.3189013831140122e-05)
SIN = (-0.16666656730445154, 0.008333010303754999, -0.00019806200404944314, 2.5992746473408684e-06)


def dot_nt(left, right):
    return lax.dot_general(
        left, right, (((1,), (1,)), ((), ())), preferred_element_type=jnp.float32
    )


def pair_terms(target, source, wave, sign):
    diff = [target[a] - source[a] for a in range(3)]
    squared = diff[0] * diff[0] + diff[1] * diff[1] + diff[2] * diff[2]
    present = squared > 0.0
    squared = jnp.where(present, squared, 1.0)
    inverse = lax.rsqrt(squared)
    phase = squared * inverse * wave
    turns = jnp.floor(phase * (1.0 / math.pi) + 0.5)
    rest = (phase - turns * PI_HIGH) - turns * PI_LOW
    half_turns = turns * 0.5
    odd = half_turns - jnp.floor(half_turns)
    amplitude = jnp.where(present, inverse * 0.5, 0.0) * (1.0 - 4.0 * odd)
    rest_sq = rest * rest
    cosine = 1.0 + rest_sq * (
        COS[0] + rest_sq * (COS[1] + rest_sq * (COS[2] + rest_sq * COS[3]))
    )
    sine = rest + rest * rest_sq * (
        SIN[0] + rest_sq * (SIN[1] + rest_sq * (SIN[2] + rest_sq * SIN[3]))
    )
    cosine = cosine * amplitude
    sine = sine * amplitude
    unit = [d * inverse for d in diff]
    z = inverse if wave == 1.0 else inverse * (1.0 / wave)
    z_sq = z * z
    one = 1.0 - z_sq
    three = 3.0 * z_sq - 1.0
    cos_z = cosine * z
    sin_z = sine * z
    same_real = cosine * one - sin_z
    same_imag = sine * one + cos_z
    along_real = cosine * three + 3.0 * sin_z
    along_imag = sine * three - 3.0 * cos_z
    if sign < 0:
        same_imag = -same_imag
        along_imag = -along_imag
    return unit, (same_real, same_imag), (along_real, along_imag)


def body(
    slabs,
    fields_in,
    incident_in,
    pos_in,
    chi_in,
    skel_in,
    near_ref,
    vf_in,
    vh_in,
    fund_ref,
    adj_ref,
    incident_ref,
    chi_ref,
    skel_ref,
    vf_ref,
    vh_ref,
    target_ref,
    pos_all,
    skel_all,
    raw_first,
    raw_second,
    chg_first,
    chg_second,
    part_out,
    part_in,
    near_k,
    far_k,
    acc_ref,
    pos_send,
    pos_recv,
    skel_send,
    skel_recv,
    raw_send,
    raw_recv,
    chg_send,
    chg_recv,
    part_send,
    part_recv,
    load_sem,
):
    tiles = slabs // 2
    raw_all = (raw_first, raw_second)
    chg_all = (chg_first, chg_second)
    group = lax.axis_index("groups")
    me = lax.axis_index("tiles")
    own_tile = lax.div(me, 2)
    my_half = lax.rem(me, 2)
    partner = own_tile * 2 + (1 - my_half)

    def peer(step):
        return lax.rem(me + 2 * step, slabs)

    def wrap_tile(t):
        return lax.rem(t + tiles, tiles)

    near_peers = [(d, wrap_tile(own_tile + d) * 2 + my_half) for d in (-1, 1, -2, 2)]
    own_slot = 4 + my_half

    def slot_of(d, half):
        return (d + 2) * 2 + half

    barrier = pltpu.get_barrier_semaphore()

    def greet(step, carry):
        pl.semaphore_signal(
            barrier, inc=1, device_id=(group, peer(step)), device_id_type=pl.DeviceIdType.MESH
        )
        return carry

    pl.semaphore_signal(
        barrier, inc=1, device_id=(group, partner), device_id_type=pl.DeviceIdType.MESH
    )
    lax.fori_loop(1, tiles, greet, 0)

    def copy(src, dst, send, recv, slab):
        return pltpu.make_async_remote_copy(
            src_ref=src,
            dst_ref=dst,
            send_sem=send,
            recv_sem=recv,
            device_id=(group, slab),
            device_id_type=pl.DeviceIdType.MESH,
        )

    def partial(phase, fields, v_ref):
        half = 1 - my_half
        part_out[phase, half] = dot_nt(fields, v_ref[pl.ds(pl.multiple_of(half * HALF, HALF), HALF), :])
        part_copy(phase).start()
        half = my_half
        part_out[phase, half] = dot_nt(fields, v_ref[pl.ds(pl.multiple_of(half * HALF, HALF), HALF), :])

    def part_copy(phase):
        return copy(
            part_out.at[phase, 1 - my_half],
            part_in.at[phase],
            part_send.at[phase],
            part_recv.at[phase],
            partner,
        )

    def near_sends(buffer, send, recv):
        for number, (d, slab) in enumerate(near_peers):
            slot = slot_of(-d, my_half)
            copy(buffer.at[own_slot], buffer.at[slot], send.at[1 + number], recv.at[slot], slab).start()

    def partner_send(buffer, send, recv):
        copy(buffer.at[own_slot], buffer.at[own_slot], send.at[0], recv.at[own_slot], partner).start()

    def near_wait(buffer, send, recv, slot):
        copy(buffer.at[own_slot], buffer.at[slot], send.at[0], recv.at[slot], partner).wait_recv()

    def near_forward(buffer, send, recv):
        for number, (d, slab) in enumerate(near_peers):
            slot = slot_of(d, my_half)
            near_wait(buffer, send, recv, slot)
            copy(buffer.at[slot], buffer.at[slot], send.at[5 + number], recv.at[slot], partner).start()

    def near_arrive(buffer, send, recv):
        for d, slab in near_peers:
            near_wait(buffer, send, recv, slot_of(d, 1 - my_half))

    def near_sent(buffer, send, recv):
        for number in range(9):
            copy(
                buffer.at[own_slot], buffer.at[own_slot], send.at[number], recv.at[own_slot], partner
            ).wait_send()

    def loop(act):
        def go(step, carry):
            act(step)
            return carry

        lax.fori_loop(1, tiles, go, 0)

    def far_sends(buffer, send, recv):
        copy(buffer.at[me], buffer.at[me], send.at[0], recv.at[me], partner).start()
        loop(
            lambda step: copy(
                buffer.at[me], buffer.at[me], send.at[step], recv.at[me], peer(step)
            ).start()
        )

    def far_wait(buffer, send, recv, slab):
        copy(buffer.at[me], buffer.at[slab], send.at[0], recv.at[slab], partner).wait_recv()

    def far_forward(buffer, send, recv):
        def act(step):
            slab = peer(step)
            far_wait(buffer, send, recv, slab)
            copy(
                buffer.at[slab], buffer.at[slab], send.at[tiles - 1 + step], recv.at[slab], partner
            ).start()

        loop(act)

    def far_arrive(buffer, send, recv):
        far_wait(buffer, send, recv, partner)
        loop(lambda step: far_wait(buffer, send, recv, lax.rem(partner + 2 * step, slabs)))

    def far_sent(buffer, send, recv):
        def go(number, carry):
            copy(buffer.at[me], buffer.at[me], send.at[number], recv.at[me], partner).wait_send()
            return carry

        lax.fori_loop(0, slabs - 1, go, 0)

    pos_set = (pos_all, pos_send, pos_recv)
    skel_set = (skel_all, skel_send, skel_recv)
    raw_set = [(raw_all[p], raw_send.at[p], raw_recv.at[p]) for p in range(2)]
    chg_set = [(chg_all[p], chg_send.at[p], chg_recv.at[p]) for p in range(2)]

    def send_charges(phase):
        part_copy(phase).wait_recv()
        summed = part_out[phase, my_half] + part_in[phase]
        chg_all[phase][me] = summed.astype(jnp.bfloat16)
        far_sends(*chg_set[phase])

    first, second = near_ref[0, 0], near_ref[0, 1]

    def near_slot(t):
        d = t - own_tile + 2
        d = jnp.where(d < 0, d + tiles, d)
        d = jnp.where(d >= tiles, d - tiles, d)
        return jnp.minimum(jnp.maximum(d, 0), 4)

    def near_place(place):
        return near_slot(
            jnp.where(place == 0, own_tile, jnp.where(place == 1, first, second))
        )

    low = jnp.minimum(own_tile, jnp.minimum(first, second))
    high = jnp.maximum(own_tile, jnp.maximum(first, second))
    middle = own_tile + first + second - low - high

    def far_tile(number):
        t = jnp.where(number >= low, number + 1, number)
        t = jnp.where(t >= middle, t + 1, t)
        return jnp.minimum(jnp.where(t >= high, t + 1, t), tiles - 1)

    def near_eval(place, half, wave, sign, own=False):
        slot = 4 + half if own else near_place(place) * 2 + half
        source = [pos_all[slot, a] for a in range(3)]
        for chunk in range(HALF // CHUNK):
            rows = slice(chunk * CHUNK, (chunk + 1) * CHUNK)
            target = [target_ref[a, rows, :] for a in range(3)]
            unit, same, along = pair_terms(target, source, wave, sign)
            for part in range(2):
                scaled = [along[part] * unit[a] for a in range(3)]
                for a in range(3):
                    for b in range(a, 3):
                        value = scaled[a] * unit[b]
                        if a == b:
                            value = value + same[part]
                        value = value.astype(jnp.bfloat16)
                        for p, q in [(a, b), (b, a)][: 1 + (a != b)]:
                            start = part * UNKNOWNS + p * HALF + chunk * CHUNK
                            near_k[
                                place * 2 + half, start : start + CHUNK, q * HALF : (q + 1) * HALF
                            ] = value

    def far_eval(number, half, wave, sign):
        block = skel_all[far_tile(number) * 2 + half]
        source = [block[a : a + 1, :] for a in range(3)]
        which = [block[3 + a : 4 + a, :] for a in range(3)]
        for chunk in range(HALF // CHUNK):
            rows = slice(chunk * CHUNK, (chunk + 1) * CHUNK)
            target = [target_ref[a, rows, :] for a in range(3)]
            unit, same, along = pair_terms(target, source, wave, sign)
            projected = unit[0] * which[0] + unit[1] * which[1] + unit[2] * which[2]
            for part in range(2):
                scaled = along[part] * projected
                for a in range(3):
                    value = scaled * unit[a] + same[part] * which[a]
                    start = part * UNKNOWNS + a * HALF + chunk * CHUNK
                    far_k[number * 2 + half, start : start + CHUNK, :] = value.astype(jnp.bfloat16)

    def eval_near_others(wave, sign):
        def go(index, carry):
            near_eval(lax.div(index, 2), lax.rem(index, 2), wave, sign)
            return carry

        lax.fori_loop(2, 6, go, 0)

    def eval_far(start, stop, wave, sign):
        def go(index, carry):
            far_eval(lax.div(index, 2), lax.rem(index, 2), wave, sign)
            return carry

        lax.fori_loop(2 * start, 2 * stop, go, 0)

    def multiply_own(phase):
        near_wait(*raw_set[phase], 5 - my_half)
        acc_ref[...] = dot_nt(raw_all[phase][4], near_k[0]) + dot_nt(raw_all[phase][5], near_k[1])

    def multiply_near(phase):
        def go(place, carry):
            slot = near_place(place) * 2
            acc_ref[...] += dot_nt(raw_all[phase][slot], near_k[place * 2]) + dot_nt(
                raw_all[phase][slot + 1], near_k[place * 2 + 1]
            )
            return carry

        lax.fori_loop(1, 3, go, 0)

    def multiply_far(phase):
        def go(number, carry):
            slot = far_tile(number) * 2
            charges = jnp.concatenate([chg_all[phase][slot], chg_all[phase][slot + 1]], axis=1)
            columns = jnp.concatenate([far_k[number * 2], far_k[number * 2 + 1]], axis=1)
            acc_ref[...] += dot_nt(charges, columns)
            return carry

        lax.fori_loop(0, tiles - 3, go, 0)

    def combined():
        real = acc_ref[:ANGLES, :UNKNOWNS] - acc_ref[ANGLES:, UNKNOWNS:]
        imag = acc_ref[:ANGLES, UNKNOWNS:] + acc_ref[ANGLES:, :UNKNOWNS]
        return real, imag

    loads = [
        pltpu.make_async_copy(src, dst, load_sem.at[number])
        for number, (src, dst) in enumerate(
            [
                (pos_in, pos_all.at[own_slot]),
                (fields_in, raw_all[0].at[own_slot]),
                (vf_in, vf_ref),
                (skel_in, skel_ref),
                (chi_in, chi_ref),
                (incident_in, incident_ref),
                (vh_in, vh_ref),
            ]
        )
    ]
    for load in loads:
        load.start()
    loads[0].wait()
    for a in range(3):
        target_ref[a] = jnp.broadcast_to(pos_all[own_slot, a], (HALF, HALF)).T
    near_eval(0, my_half, fund_wave, 1.0, True)
    loads[1].wait()
    loads[2].wait()
    loads[3].wait()
    pl.semaphore_wait(barrier, tiles)
    partner_send(*pos_set)
    near_sends(*pos_set)
    near_sends(*raw_set[0])
    partial(0, raw_all[0][own_slot], vf_ref)
    partner_send(*raw_set[0])

    near_wait(*pos_set, 5 - my_half)
    skeleton = skel_ref[...]
    component = jnp.where(skeleton >= 2 * POINTS, 2, jnp.where(skeleton >= POINTS, 1, 0))
    point = skeleton - component * POINTS
    lines = lax.broadcasted_iota(jnp.int32, (HALF, HALF), 0)
    masks = [lines + HALF * h == point for h in range(2)]
    packet = []
    for a in range(3):
        own_column = target_ref[a]
        other_column = jnp.broadcast_to(pos_all[5 - my_half, a], (HALF, HALF)).T
        columns = [
            jnp.where(my_half == 0, own_column, other_column),
            jnp.where(my_half == 0, other_column, own_column),
        ]
        picked = jnp.where(masks[0], columns[0], jnp.where(masks[1], columns[1], 0.0))
        packet.append(jnp.sum(picked, axis=0, keepdims=True))
    for a in range(3):
        packet.append((component == a).astype(jnp.float32))
    packet.append(jnp.zeros((2, HALF), jnp.float32))
    skel_all[me] = jnp.concatenate(packet, axis=0)
    far_sends(*skel_set)
    send_charges(0)

    near_forward(*pos_set)
    near_eval(0, 1 - my_half, fund_wave, 1.0, True)
    multiply_own(0)
    far_forward(*skel_set)
    near_arrive(*pos_set)
    eval_near_others(fund_wave, 1.0)
    near_forward(*raw_set[0])
    far_arrive(*skel_set)
    split = (tiles - 3) // 2
    eval_far(0, split, fund_wave, 1.0)
    far_forward(*chg_set[0])
    eval_far(split, tiles - 3, fund_wave, 1.0)
    near_arrive(*raw_set[0])
    multiply_near(0)
    far_arrive(*chg_set[0])
    multiply_far(0)

    loads[4].wait()
    loads[5].wait()
    loads[6].wait()
    real, imag = combined()
    real = incident_ref[:ANGLES, :].astype(jnp.float32) + real
    imag = incident_ref[ANGLES:, :].astype(jnp.float32) + imag
    fund_ref[:ANGLES, :] = real
    fund_ref[ANGLES:, :] = imag
    weights = jnp.concatenate([chi_ref[...]] * 3, axis=1)
    source = jnp.concatenate(
        [weights * (real * real - imag * imag), weights * 2.0 * real * imag], axis=0
    ).astype(jnp.bfloat16)

    raw_all[1][own_slot] = source
    near_sends(*raw_set[1])
    partial(1, source, vh_ref)
    partner_send(*raw_set[1])
    near_eval(0, my_half, harm_wave, -1.0, True)
    send_charges(1)
    near_eval(0, 1 - my_half, harm_wave, -1.0, True)
    multiply_own(1)
    eval_near_others(harm_wave, -1.0)
    near_forward(*raw_set[1])
    eval_far(0, split, harm_wave, -1.0)
    far_forward(*chg_set[1])
    eval_far(split, tiles - 3, harm_wave, -1.0)
    near_arrive(*raw_set[1])
    multiply_near(1)
    far_arrive(*chg_set[1])
    multiply_far(1)
    real, imag = combined()
    adj_ref[:ANGLES, :] = real
    adj_ref[ANGLES:, :] = imag

    near_sent(*pos_set)
    far_sent(*skel_set)
    for phase in range(2):
        part_copy(phase).wait_send()
        near_sent(*raw_set[phase])
        far_sent(*chg_set[phase])


def solution(mesh):
    slabs = mesh.shape["tiles"]
    tiles = slabs // 2
    bf16, f32 = jnp.bfloat16, jnp.float32
    dma = pltpu.SemaphoreType.DMA
    hbm = pl.BlockSpec(memory_space=pltpu.HBM)
    vmem = pl.BlockSpec(memory_space=pltpu.VMEM)

    def on_device(dipoles, incident, positions, chi, skeletons, near, vf, vh):
        fields = dipoles.reshape(ROWS, UNKNOWNS)
        out = jax.ShapeDtypeStruct((ROWS, UNKNOWNS), f32)
        fund, adj = pl.pallas_call(
            lambda *refs: body(slabs, *refs),
            out_shape=(out, out),
            in_specs=[hbm] * 5 + [pl.BlockSpec(memory_space=pltpu.SMEM)] + [hbm] * 2,
            out_specs=(vmem, vmem),
            scratch_shapes=[
                pltpu.VMEM((ROWS, UNKNOWNS), bf16),
                pltpu.VMEM((1, HALF), f32),
                pltpu.VMEM((1, HALF), jnp.int32),
                pltpu.VMEM((SKELETONS, UNKNOWNS), bf16),
                pltpu.VMEM((SKELETONS, UNKNOWNS), bf16),
                pltpu.VMEM((3, HALF, HALF), f32),
                pltpu.VMEM((10, 3, 1, HALF), f32),
                pltpu.VMEM((slabs, 8, HALF), f32),
                pltpu.VMEM((10, ROWS, UNKNOWNS), bf16),
                pltpu.VMEM((10, ROWS, UNKNOWNS), bf16),
                pltpu.VMEM((slabs, ROWS, HALF), bf16),
                pltpu.VMEM((slabs, ROWS, HALF), bf16),
                pltpu.VMEM((2, 2, ROWS, HALF), f32),
                pltpu.VMEM((2, ROWS, HALF), f32),
                pltpu.VMEM((6, 2 * UNKNOWNS, UNKNOWNS), bf16),
                pltpu.VMEM((2 * (tiles - 3), 2 * UNKNOWNS, HALF), bf16),
                pltpu.VMEM((ROWS, 2 * UNKNOWNS), f32),
                dma((9,)),
                dma((10,)),
                dma((slabs,)),
                dma((slabs,)),
                dma((2, 9)),
                dma((2, 10)),
                dma((2, slabs)),
                dma((2, slabs)),
                dma((2,)),
                dma((2,)),
                dma((7,)),
            ],
            compiler_params=pltpu.CompilerParams(
                collective_id=0, has_side_effects=True, vmem_limit_bytes=VMEM
            ),
            name="images",
        )(
            fields,
            incident.reshape(ROWS, UNKNOWNS),
            jnp.transpose(positions, (1, 0, 2)),
            chi,
            skeletons,
            near,
            vf[0],
            vh[0],
        )
        shape = (1, 2, ANGLES, UNKNOWNS)
        return fund.reshape(shape), adj.reshape(shape)

    row = ("groups", "tiles")
    in_specs = (
        P(row, None, None, None),
        P(row, None, None, None),
        P(row, None, None),
        P(row, None),
        P(row, None),
        P(row, None),
        P(row, None, None),
        P(row, None, None),
    )
    out_specs = (P(row, None, None, None), P(row, None, None, None))
    return jax.shard_map(
        on_device, mesh=mesh, in_specs=in_specs, out_specs=out_specs, check_vma=False
    )
```

```python
import math

import jax
import jax.numpy as jnp
from jax import lax
from jax.experimental import pallas as pl
from jax.experimental.pallas import tpu as pltpu
from jax.sharding import PartitionSpec as P

POINTS = 256
SKELETONS = 256
ANGLES = 32
HALF = 128
ROWS = 2 * ANGLES
UNKNOWNS = 3 * HALF
CHUNK = 16
VMEM = 64 * 2**20 - 64 * 1024

fund_wave = 0.5
harm_wave = 1.0

PI_HIGH = 3.140625
PI_LOW = math.pi - 3.140625
COS = (-0.4999993031990062, 0.04166394733655344, -0.0013855657175274386, 2.3189013831140122e-05)
SIN = (-0.16666656730445154, 0.008333010303754999, -0.00019806200404944314, 2.5992746473408684e-06)


def dot_nt(left, right):
    return lax.dot_general(
        left, right, (((1,), (1,)), ((), ())), preferred_element_type=jnp.float32
    )


def pair_terms(target, source, wave, sign):
    diff = [target[a] - source[a] for a in range(3)]
    squared = diff[0] * diff[0] + diff[1] * diff[1] + diff[2] * diff[2]
    present = squared > 0.0
    squared = jnp.where(present, squared, 1.0)
    inverse = lax.rsqrt(squared)
    phase = squared * inverse * wave
    turns = jnp.floor(phase * (1.0 / math.pi) + 0.5)
    rest = (phase - turns * PI_HIGH) - turns * PI_LOW
    half_turns = turns * 0.5
    odd = half_turns - jnp.floor(half_turns)
    amplitude = jnp.where(present, inverse * 0.5, 0.0) * (1.0 - 4.0 * odd)
    rest_sq = rest * rest
    cosine = 1.0 + rest_sq * (
        COS[0] + rest_sq * (COS[1] + rest_sq * (COS[2] + rest_sq * COS[3]))
    )
    sine = rest + rest * rest_sq * (
        SIN[0] + rest_sq * (SIN[1] + rest_sq * (SIN[2] + rest_sq * SIN[3]))
    )
    cosine = cosine * amplitude
    sine = sine * amplitude
    unit = [d * inverse for d in diff]
    z = inverse if wave == 1.0 else inverse * (1.0 / wave)
    z_sq = z * z
    one = 1.0 - z_sq
    three = 3.0 * z_sq - 1.0
    cos_z = cosine * z
    sin_z = sine * z
    same_real = cosine * one - sin_z
    same_imag = sine * one + cos_z
    along_real = cosine * three + 3.0 * sin_z
    along_imag = sine * three - 3.0 * cos_z
    if sign < 0:
        same_imag = -same_imag
        along_imag = -along_imag
    return unit, (same_real, same_imag), (along_real, along_imag)


def body(
    slabs,
    fields_in,
    incident_in,
    pos_in,
    chi_in,
    skel_in,
    near_ref,
    vf_in,
    vh_in,
    fund_ref,
    adj_ref,
    incident_ref,
    chi_ref,
    skel_ref,
    vf_ref,
    vh_ref,
    target_ref,
    pos_all,
    skel_all,
    raw_first,
    raw_second,
    chg_first,
    chg_second,
    part_out,
    part_in,
    near_k,
    far_k,
    acc_ref,
    pos_send,
    pos_recv,
    skel_send,
    skel_recv,
    raw_send,
    raw_recv,
    chg_send,
    chg_recv,
    part_send,
    part_recv,
    load_sem,
):
    tiles = slabs // 2
    raw_all = (raw_first, raw_second)
    chg_all = (chg_first, chg_second)
    group = lax.axis_index("groups")
    me = lax.axis_index("tiles")
    own_tile = lax.div(me, 2)
    my_half = lax.rem(me, 2)
    partner = own_tile * 2 + (1 - my_half)

    def peer(step):
        return lax.rem(me + 2 * step, slabs)

    def wrap_tile(t):
        return lax.rem(t + tiles, tiles)

    near_peers = [(d, wrap_tile(own_tile + d) * 2 + my_half) for d in (-1, 1, -2, 2)]
    own_slot = 4 + my_half

    def slot_of(d, half):
        return (d + 2) * 2 + half

    barrier = pltpu.get_barrier_semaphore()

    def greet(step, carry):
        pl.semaphore_signal(
            barrier, inc=1, device_id=(group, peer(step)), device_id_type=pl.DeviceIdType.MESH
        )
        return carry

    pl.semaphore_signal(
        barrier, inc=1, device_id=(group, partner), device_id_type=pl.DeviceIdType.MESH
    )
    lax.fori_loop(1, tiles, greet, 0)

    def copy(src, dst, send, recv, slab):
        return pltpu.make_async_remote_copy(
            src_ref=src,
            dst_ref=dst,
            send_sem=send,
            recv_sem=recv,
            device_id=(group, slab),
            device_id_type=pl.DeviceIdType.MESH,
        )

    def partial(phase, fields, v_ref):
        half = 1 - my_half
        part_out[phase, half] = dot_nt(fields, v_ref[pl.ds(pl.multiple_of(half * HALF, HALF), HALF), :])
        part_copy(phase).start()
        half = my_half
        part_out[phase, half] = dot_nt(fields, v_ref[pl.ds(pl.multiple_of(half * HALF, HALF), HALF), :])

    def part_copy(phase):
        return copy(
            part_out.at[phase, 1 - my_half],
            part_in.at[phase],
            part_send.at[phase],
            part_recv.at[phase],
            partner,
        )

    def near_sends(buffer, send, recv):
        for number, (d, slab) in enumerate(near_peers):
            slot = slot_of(-d, my_half)
            copy(buffer.at[own_slot], buffer.at[slot], send.at[1 + number], recv.at[slot], slab).start()

    def partner_send(buffer, send, recv):
        copy(buffer.at[own_slot], buffer.at[own_slot], send.at[0], recv.at[own_slot], partner).start()

    def near_wait(buffer, send, recv, slot):
        copy(buffer.at[own_slot], buffer.at[slot], send.at[0], recv.at[slot], partner).wait_recv()

    def near_forward(buffer, send, recv):
        for number, (d, slab) in enumerate(near_peers):
            slot = slot_of(d, my_half)
            near_wait(buffer, send, recv, slot)
            copy(buffer.at[slot], buffer.at[slot], send.at[5 + number], recv.at[slot], partner).start()

    def near_arrive(buffer, send, recv):
        for d, slab in near_peers:
            near_wait(buffer, send, recv, slot_of(d, 1 - my_half))

    def near_sent(buffer, send, recv):
        for number in range(9):
            copy(
                buffer.at[own_slot], buffer.at[own_slot], send.at[number], recv.at[own_slot], partner
            ).wait_send()

    def loop(act):
        def go(step, carry):
            act(step)
            return carry

        lax.fori_loop(1, tiles, go, 0)

    def far_sends(buffer, send, recv):
        copy(buffer.at[me], buffer.at[me], send.at[0], recv.at[me], partner).start()
        loop(
            lambda step: copy(
                buffer.at[me], buffer.at[me], send.at[step], recv.at[me], peer(step)
            ).start()
        )

    def far_wait(buffer, send, recv, slab):
        copy(buffer.at[me], buffer.at[slab], send.at[0], recv.at[slab], partner).wait_recv()

    def far_forward(buffer, send, recv):
        def act(step):
            slab = peer(step)
            far_wait(buffer, send, recv, slab)
            copy(
                buffer.at[slab], buffer.at[slab], send.at[tiles - 1 + step], recv.at[slab], partner
            ).start()

        loop(act)

    def far_arrive(buffer, send, recv):
        far_wait(buffer, send, recv, partner)
        loop(lambda step: far_wait(buffer, send, recv, lax.rem(partner + 2 * step, slabs)))

    def far_sent(buffer, send, recv):
        def go(number, carry):
            copy(buffer.at[me], buffer.at[me], send.at[number], recv.at[me], partner).wait_send()
            return carry

        lax.fori_loop(0, slabs - 1, go, 0)

    pos_set = (pos_all, pos_send, pos_recv)
    skel_set = (skel_all, skel_send, skel_recv)
    raw_set = [(raw_all[p], raw_send.at[p], raw_recv.at[p]) for p in range(2)]
    chg_set = [(chg_all[p], chg_send.at[p], chg_recv.at[p]) for p in range(2)]

    def send_charges(phase):
        part_copy(phase).wait_recv()
        summed = part_out[phase, my_half] + part_in[phase]
        chg_all[phase][me] = summed.astype(jnp.bfloat16)
        far_sends(*chg_set[phase])

    first, second = near_ref[0, 0], near_ref[0, 1]

    def near_slot(t):
        d = t - own_tile + 2
        d = jnp.where(d < 0, d + tiles, d)
        d = jnp.where(d >= tiles, d - tiles, d)
        return jnp.minimum(jnp.maximum(d, 0), 4)

    def near_place(place):
        return near_slot(
            jnp.where(place == 0, own_tile, jnp.where(place == 1, first, second))
        )

    low = jnp.minimum(own_tile, jnp.minimum(first, second))
    high = jnp.maximum(own_tile, jnp.maximum(first, second))
    middle = own_tile + first + second - low - high

    def far_tile(number):
        t = jnp.where(number >= low, number + 1, number)
        t = jnp.where(t >= middle, t + 1, t)
        return jnp.minimum(jnp.where(t >= high, t + 1, t), tiles - 1)

    def near_eval(place, half, wave, sign, own=False):
        slot = 4 + half if own else near_place(place) * 2 + half
        source = [pos_all[slot, a] for a in range(3)]
        for chunk in range(HALF // CHUNK):
            rows = slice(chunk * CHUNK, (chunk + 1) * CHUNK)
            target = [target_ref[a, rows, :] for a in range(3)]
            unit, same, along = pair_terms(target, source, wave, sign)
            for part in range(2):
                scaled = [along[part] * unit[a] for a in range(3)]
                for a in range(3):
                    for b in range(a, 3):
                        value = scaled[a] * unit[b]
                        if a == b:
                            value = value + same[part]
                        value = value.astype(jnp.bfloat16)
                        for p, q in [(a, b), (b, a)][: 1 + (a != b)]:
                            start = part * UNKNOWNS + p * HALF + chunk * CHUNK
                            near_k[
                                place * 2 + half, start : start + CHUNK, q * HALF : (q + 1) * HALF
                            ] = value

    def far_eval(number, half, wave, sign):
        block = skel_all[far_tile(number) * 2 + half]
        source = [block[a : a + 1, :] for a in range(3)]
        which = [block[3 + a : 4 + a, :] for a in range(3)]
        for chunk in range(HALF // CHUNK):
            rows = slice(chunk * CHUNK, (chunk + 1) * CHUNK)
            target = [target_ref[a, rows, :] for a in range(3)]
            unit, same, along = pair_terms(target, source, wave, sign)
            projected = unit[0] * which[0] + unit[1] * which[1] + unit[2] * which[2]
            for part in range(2):
                scaled = along[part] * projected
                for a in range(3):
                    value = scaled * unit[a] + same[part] * which[a]
                    start = part * UNKNOWNS + a * HALF + chunk * CHUNK
                    far_k[number * 2 + half, start : start + CHUNK, :] = value.astype(jnp.bfloat16)

    def eval_near_others(wave, sign):
        def go(index, carry):
            near_eval(lax.div(index, 2), lax.rem(index, 2), wave, sign)
            return carry

        lax.fori_loop(2, 6, go, 0)

    def eval_far(start, stop, wave, sign):
        def go(index, carry):
            far_eval(lax.div(index, 2), lax.rem(index, 2), wave, sign)
            return carry

        lax.fori_loop(2 * start, 2 * stop, go, 0)

    def multiply_own(phase):
        near_wait(*raw_set[phase], 5 - my_half)
        acc_ref[...] = dot_nt(raw_all[phase][4], near_k[0]) + dot_nt(raw_all[phase][5], near_k[1])

    def multiply_near(phase):
        def go(place, carry):
            slot = near_place(place) * 2
            acc_ref[...] += dot_nt(raw_all[phase][slot], near_k[place * 2]) + dot_nt(
                raw_all[phase][slot + 1], near_k[place * 2 + 1]
            )
            return carry

        lax.fori_loop(1, 3, go, 0)

    def multiply_far(phase):
        def go(number, carry):
            slot = far_tile(number) * 2
            charges = jnp.concatenate([chg_all[phase][slot], chg_all[phase][slot + 1]], axis=1)
            columns = jnp.concatenate([far_k[number * 2], far_k[number * 2 + 1]], axis=1)
            acc_ref[...] += dot_nt(charges, columns)
            return carry

        lax.fori_loop(0, tiles - 3, go, 0)

    def combined():
        real = acc_ref[:ANGLES, :UNKNOWNS] - acc_ref[ANGLES:, UNKNOWNS:]
        imag = acc_ref[:ANGLES, UNKNOWNS:] + acc_ref[ANGLES:, :UNKNOWNS]
        return real, imag

    loads = [
        pltpu.make_async_copy(src, dst, load_sem.at[number])
        for number, (src, dst) in enumerate(
            [
                (pos_in, pos_all.at[own_slot]),
                (fields_in, raw_all[0].at[own_slot]),
                (vf_in, vf_ref),
                (skel_in, skel_ref),
                (chi_in, chi_ref),
                (incident_in, incident_ref),
                (vh_in, vh_ref),
            ]
        )
    ]
    for load in loads:
        load.start()
    loads[0].wait()
    for a in range(3):
        target_ref[a] = jnp.broadcast_to(pos_all[own_slot, a], (HALF, HALF)).T
    near_eval(0, my_half, fund_wave, 1.0, True)
    loads[1].wait()
    loads[2].wait()
    loads[3].wait()
    pl.semaphore_wait(barrier, tiles)
    partner_send(*pos_set)
    near_sends(*pos_set)
    near_sends(*raw_set[0])
    partial(0, raw_all[0][own_slot], vf_ref)
    partner_send(*raw_set[0])

    near_wait(*pos_set, 5 - my_half)
    skeleton = skel_ref[...]
    component = jnp.where(skeleton >= 2 * POINTS, 2, jnp.where(skeleton >= POINTS, 1, 0))
    point = skeleton - component * POINTS
    lines = lax.broadcasted_iota(jnp.int32, (HALF, HALF), 0)
    masks = [lines + HALF * h == point for h in range(2)]
    packet = []
    for a in range(3):
        own_column = target_ref[a]
        other_column = jnp.broadcast_to(pos_all[5 - my_half, a], (HALF, HALF)).T
        columns = [
            jnp.where(my_half == 0, own_column, other_column),
            jnp.where(my_half == 0, other_column, own_column),
        ]
        picked = jnp.where(masks[0], columns[0], jnp.where(masks[1], columns[1], 0.0))
        packet.append(jnp.sum(picked, axis=0, keepdims=True))
    for a in range(3):
        packet.append((component == a).astype(jnp.float32))
    packet.append(jnp.zeros((2, HALF), jnp.float32))
    skel_all[me] = jnp.concatenate(packet, axis=0)
    far_sends(*skel_set)
    send_charges(0)

    near_forward(*pos_set)
    near_eval(0, 1 - my_half, fund_wave, 1.0, True)
    multiply_own(0)
    far_forward(*skel_set)
    near_arrive(*pos_set)
    eval_near_others(fund_wave, 1.0)
    near_forward(*raw_set[0])
    far_arrive(*skel_set)
    eval_far(0, tiles - 3, fund_wave, 1.0)
    near_arrive(*raw_set[0])
    multiply_near(0)
    far_forward(*chg_set[0])
    far_arrive(*chg_set[0])
    multiply_far(0)

    loads[4].wait()
    loads[5].wait()
    loads[6].wait()
    real, imag = combined()
    real = incident_ref[:ANGLES, :].astype(jnp.float32) + real
    imag = incident_ref[ANGLES:, :].astype(jnp.float32) + imag
    fund_ref[:ANGLES, :] = real
    fund_ref[ANGLES:, :] = imag
    weights = jnp.concatenate([chi_ref[...]] * 3, axis=1)
    source = jnp.concatenate(
        [weights * (real * real - imag * imag), weights * 2.0 * real * imag], axis=0
    ).astype(jnp.bfloat16)

    raw_all[1][own_slot] = source
    near_sends(*raw_set[1])
    partial(1, source, vh_ref)
    partner_send(*raw_set[1])
    near_eval(0, my_half, harm_wave, -1.0, True)
    send_charges(1)
    near_eval(0, 1 - my_half, harm_wave, -1.0, True)
    multiply_own(1)
    eval_near_others(harm_wave, -1.0)
    near_forward(*raw_set[1])
    eval_far(0, tiles - 3, harm_wave, -1.0)
    near_arrive(*raw_set[1])
    multiply_near(1)
    far_forward(*chg_set[1])
    far_arrive(*chg_set[1])
    multiply_far(1)
    real, imag = combined()
    adj_ref[:ANGLES, :] = real
    adj_ref[ANGLES:, :] = imag

    near_sent(*pos_set)
    far_sent(*skel_set)
    for phase in range(2):
        part_copy(phase).wait_send()
        near_sent(*raw_set[phase])
        far_sent(*chg_set[phase])


def solution(mesh):
    slabs = mesh.shape["tiles"]
    tiles = slabs // 2
    bf16, f32 = jnp.bfloat16, jnp.float32
    dma = pltpu.SemaphoreType.DMA
    hbm = pl.BlockSpec(memory_space=pltpu.HBM)
    vmem = pl.BlockSpec(memory_space=pltpu.VMEM)

    def on_device(dipoles, incident, positions, chi, skeletons, near, vf, vh):
        fields = dipoles.reshape(ROWS, UNKNOWNS)
        out = jax.ShapeDtypeStruct((ROWS, UNKNOWNS), f32)
        fund, adj = pl.pallas_call(
            lambda *refs: body(slabs, *refs),
            out_shape=(out, out),
            in_specs=[hbm] * 5 + [pl.BlockSpec(memory_space=pltpu.SMEM)] + [hbm] * 2,
            out_specs=(vmem, vmem),
            scratch_shapes=[
                pltpu.VMEM((ROWS, UNKNOWNS), bf16),
                pltpu.VMEM((1, HALF), f32),
                pltpu.VMEM((1, HALF), jnp.int32),
                pltpu.VMEM((SKELETONS, UNKNOWNS), bf16),
                pltpu.VMEM((SKELETONS, UNKNOWNS), bf16),
                pltpu.VMEM((3, HALF, HALF), f32),
                pltpu.VMEM((10, 3, 1, HALF), f32),
                pltpu.VMEM((slabs, 8, HALF), f32),
                pltpu.VMEM((10, ROWS, UNKNOWNS), bf16),
                pltpu.VMEM((10, ROWS, UNKNOWNS), bf16),
                pltpu.VMEM((slabs, ROWS, HALF), bf16),
                pltpu.VMEM((slabs, ROWS, HALF), bf16),
                pltpu.VMEM((2, 2, ROWS, HALF), f32),
                pltpu.VMEM((2, ROWS, HALF), f32),
                pltpu.VMEM((6, 2 * UNKNOWNS, UNKNOWNS), bf16),
                pltpu.VMEM((2 * (tiles - 3), 2 * UNKNOWNS, HALF), bf16),
                pltpu.VMEM((ROWS, 2 * UNKNOWNS), f32),
                dma((9,)),
                dma((10,)),
                dma((slabs,)),
                dma((slabs,)),
                dma((2, 9)),
                dma((2, 10)),
                dma((2, slabs)),
                dma((2, slabs)),
                dma((2,)),
                dma((2,)),
                dma((7,)),
            ],
            compiler_params=pltpu.CompilerParams(
                collective_id=0, has_side_effects=True, vmem_limit_bytes=VMEM
            ),
            name="images",
        )(
            fields,
            incident.reshape(ROWS, UNKNOWNS),
            jnp.transpose(positions, (1, 0, 2)),
            chi,
            skeletons,
            near,
            vf[0],
            vh[0],
        )
        shape = (1, 2, ANGLES, UNKNOWNS)
        return fund.reshape(shape), adj.reshape(shape)

    row = ("groups", "tiles")
    in_specs = (
        P(row, None, None, None),
        P(row, None, None, None),
        P(row, None, None),
        P(row, None),
        P(row, None),
        P(row, None),
        P(row, None, None),
        P(row, None, None),
    )
    out_specs = (P(row, None, None, None), P(row, None, None, None))
    return jax.shard_map(
        on_device, mesh=mesh, in_specs=in_specs, out_specs=out_specs, check_vma=False
    )
```

```python
import math

import jax
import jax.numpy as jnp
from jax import lax
from jax.experimental import pallas as pl
from jax.experimental.pallas import tpu as pltpu
from jax.sharding import PartitionSpec as P

POINTS = 256
SKELETONS = 256
ANGLES = 32
HALF = 128
ROWS = 2 * ANGLES
UNKNOWNS = 3 * HALF
CHUNK = 16
VMEM = 64 * 2**20 - 64 * 1024

fund_wave = 0.5
harm_wave = 1.0

PI_HIGH = 3.140625
PI_LOW = math.pi - 3.140625
COS = (-0.4999993031990062, 0.04166394733655344, -0.0013855657175274386, 2.3189013831140122e-05)
SIN = (-0.16666656730445154, 0.008333010303754999, -0.00019806200404944314, 2.5992746473408684e-06)


def dot_nt(left, right):
    return lax.dot_general(
        left, right, (((1,), (1,)), ((), ())), preferred_element_type=jnp.float32
    )


def pair_terms(target, source, wave, sign):
    diff = [target[a] - source[a] for a in range(3)]
    squared = diff[0] * diff[0] + diff[1] * diff[1] + diff[2] * diff[2]
    present = squared > 0.0
    squared = jnp.where(present, squared, 1.0)
    inverse = lax.rsqrt(squared)
    phase = squared * inverse * wave
    turns = jnp.floor(phase * (1.0 / math.pi) + 0.5)
    rest = (phase - turns * PI_HIGH) - turns * PI_LOW
    half_turns = turns * 0.5
    odd = half_turns - jnp.floor(half_turns)
    amplitude = jnp.where(present, inverse * 0.5, 0.0) * (1.0 - 4.0 * odd)
    rest_sq = rest * rest
    cosine = 1.0 + rest_sq * (
        COS[0] + rest_sq * (COS[1] + rest_sq * (COS[2] + rest_sq * COS[3]))
    )
    sine = rest + rest * rest_sq * (
        SIN[0] + rest_sq * (SIN[1] + rest_sq * (SIN[2] + rest_sq * SIN[3]))
    )
    cosine = cosine * amplitude
    sine = sine * amplitude
    unit = [d * inverse for d in diff]
    z = inverse if wave == 1.0 else inverse * (1.0 / wave)
    z_sq = z * z
    one = 1.0 - z_sq
    three = 3.0 * z_sq - 1.0
    cos_z = cosine * z
    sin_z = sine * z
    same_real = cosine * one - sin_z
    same_imag = sine * one + cos_z
    along_real = cosine * three + 3.0 * sin_z
    along_imag = sine * three - 3.0 * cos_z
    if sign < 0:
        same_imag = -same_imag
        along_imag = -along_imag
    return unit, (same_real, same_imag), (along_real, along_imag)


def body(
    slabs,
    fields_in,
    incident_in,
    pos_in,
    chi_in,
    skel_in,
    near_ref,
    vf_in,
    vh_in,
    fund_ref,
    adj_ref,
    incident_ref,
    chi_ref,
    skel_ref,
    vf_ref,
    vh_ref,
    target_ref,
    pos_all,
    skel_all,
    raw_first,
    raw_second,
    chg_first,
    chg_second,
    part_out,
    part_in,
    near_k,
    far_k,
    acc_ref,
    pos_send,
    pos_recv,
    skel_send,
    skel_recv,
    raw_send,
    raw_recv,
    chg_send,
    chg_recv,
    part_send,
    part_recv,
    load_sem,
):
    tiles = slabs // 2
    raw_all = (raw_first, raw_second)
    chg_all = (chg_first, chg_second)
    group = lax.axis_index("groups")
    me = lax.axis_index("tiles")
    own_tile = lax.div(me, 2)
    my_half = lax.rem(me, 2)
    partner = own_tile * 2 + (1 - my_half)

    def peer(step):
        return lax.rem(me + 2 * step, slabs)

    def wrap_tile(t):
        return lax.rem(t + tiles, tiles)

    near_peers = [(d, wrap_tile(own_tile + d) * 2 + my_half) for d in (-1, 1, -2, 2)]
    own_slot = 4 + my_half

    def slot_of(d, half):
        return (d + 2) * 2 + half

    barrier = pltpu.get_barrier_semaphore()

    def greet(step, carry):
        pl.semaphore_signal(
            barrier, inc=1, device_id=(group, peer(step)), device_id_type=pl.DeviceIdType.MESH
        )
        return carry

    pl.semaphore_signal(
        barrier, inc=1, device_id=(group, partner), device_id_type=pl.DeviceIdType.MESH
    )
    lax.fori_loop(1, tiles, greet, 0)

    def copy(src, dst, send, recv, slab):
        return pltpu.make_async_remote_copy(
            src_ref=src,
            dst_ref=dst,
            send_sem=send,
            recv_sem=recv,
            device_id=(group, slab),
            device_id_type=pl.DeviceIdType.MESH,
        )

    def partial(phase, fields, v_ref):
        half = 1 - my_half
        part_out[phase, half] = dot_nt(fields, v_ref[pl.ds(pl.multiple_of(half * HALF, HALF), HALF), :])
        part_copy(phase).start()
        half = my_half
        part_out[phase, half] = dot_nt(fields, v_ref[pl.ds(pl.multiple_of(half * HALF, HALF), HALF), :])

    def part_copy(phase):
        return copy(
            part_out.at[phase, 1 - my_half],
            part_in.at[phase],
            part_send.at[phase],
            part_recv.at[phase],
            partner,
        )

    def near_sends(buffer, send, recv):
        for number, (d, slab) in enumerate(near_peers):
            slot = slot_of(-d, my_half)
            copy(buffer.at[own_slot], buffer.at[slot], send.at[1 + number], recv.at[slot], slab).start()

    def partner_send(buffer, send, recv):
        copy(buffer.at[own_slot], buffer.at[own_slot], send.at[0], recv.at[own_slot], partner).start()

    def near_wait(buffer, send, recv, slot):
        copy(buffer.at[own_slot], buffer.at[slot], send.at[0], recv.at[slot], partner).wait_recv()

    def near_forward(buffer, send, recv):
        for number, (d, slab) in enumerate(near_peers):
            slot = slot_of(d, my_half)
            near_wait(buffer, send, recv, slot)
            copy(buffer.at[slot], buffer.at[slot], send.at[5 + number], recv.at[slot], partner).start()

    def near_arrive(buffer, send, recv):
        for d, slab in near_peers:
            near_wait(buffer, send, recv, slot_of(d, 1 - my_half))

    def near_sent(buffer, send, recv):
        for number in range(9):
            copy(
                buffer.at[own_slot], buffer.at[own_slot], send.at[number], recv.at[own_slot], partner
            ).wait_send()

    def loop(act):
        def go(step, carry):
            act(step)
            return carry

        lax.fori_loop(1, tiles, go, 0)

    def far_sends(buffer, send, recv):
        copy(buffer.at[me], buffer.at[me], send.at[0], recv.at[me], partner).start()
        loop(
            lambda step: copy(
                buffer.at[me], buffer.at[me], send.at[step], recv.at[me], peer(step)
            ).start()
        )

    def far_wait(buffer, send, recv, slab):
        copy(buffer.at[me], buffer.at[slab], send.at[0], recv.at[slab], partner).wait_recv()

    def far_forward(buffer, send, recv):
        def act(step):
            slab = peer(step)
            far_wait(buffer, send, recv, slab)
            copy(
                buffer.at[slab], buffer.at[slab], send.at[tiles - 1 + step], recv.at[slab], partner
            ).start()

        loop(act)

    def far_arrive(buffer, send, recv):
        far_wait(buffer, send, recv, partner)
        loop(lambda step: far_wait(buffer, send, recv, lax.rem(partner + 2 * step, slabs)))

    def far_sent(buffer, send, recv):
        def go(number, carry):
            copy(buffer.at[me], buffer.at[me], send.at[number], recv.at[me], partner).wait_send()
            return carry

        lax.fori_loop(0, slabs - 1, go, 0)

    pos_set = (pos_all, pos_send, pos_recv)
    skel_set = (skel_all, skel_send, skel_recv)
    raw_set = [(raw_all[p], raw_send.at[p], raw_recv.at[p]) for p in range(2)]
    chg_set = [(chg_all[p], chg_send.at[p], chg_recv.at[p]) for p in range(2)]

    def send_charges(phase):
        part_copy(phase).wait_recv()
        summed = part_out[phase, my_half] + part_in[phase]
        chg_all[phase][me] = summed.astype(jnp.bfloat16)
        far_sends(*chg_set[phase])

    first, second = near_ref[0, 0], near_ref[0, 1]

    def near_slot(t):
        d = t - own_tile + 2
        d = jnp.where(d < 0, d + tiles, d)
        d = jnp.where(d >= tiles, d - tiles, d)
        return jnp.minimum(jnp.maximum(d, 0), 4)

    def near_place(place):
        return near_slot(
            jnp.where(place == 0, own_tile, jnp.where(place == 1, first, second))
        )

    low = jnp.minimum(own_tile, jnp.minimum(first, second))
    high = jnp.maximum(own_tile, jnp.maximum(first, second))
    middle = own_tile + first + second - low - high

    def far_tile(number):
        t = jnp.where(number >= low, number + 1, number)
        t = jnp.where(t >= middle, t + 1, t)
        return jnp.minimum(jnp.where(t >= high, t + 1, t), tiles - 1)

    def near_eval(place, half, wave, sign, own=False):
        slot = 4 + half if own else near_place(place) * 2 + half
        source = [pos_all[slot, a] for a in range(3)]
        for chunk in range(HALF // CHUNK):
            rows = slice(chunk * CHUNK, (chunk + 1) * CHUNK)
            target = [target_ref[a, rows, :] for a in range(3)]
            unit, same, along = pair_terms(target, source, wave, sign)
            for part in range(2):
                scaled = [along[part] * unit[a] for a in range(3)]
                for a in range(3):
                    for b in range(a, 3):
                        value = scaled[a] * unit[b]
                        if a == b:
                            value = value + same[part]
                        value = value.astype(jnp.bfloat16)
                        for p, q in [(a, b), (b, a)][: 1 + (a != b)]:
                            start = part * UNKNOWNS + p * HALF + chunk * CHUNK
                            first_lane = pl.multiple_of(half * UNKNOWNS + q * HALF, HALF)
                            near_k[place, start : start + CHUNK, pl.ds(first_lane, HALF)] = value

    def far_eval(number, half, wave, sign):
        block = skel_all[far_tile(number) * 2 + half]
        source = [block[a : a + 1, :] for a in range(3)]
        which = [block[3 + a : 4 + a, :] for a in range(3)]
        for chunk in range(HALF // CHUNK):
            rows = slice(chunk * CHUNK, (chunk + 1) * CHUNK)
            target = [target_ref[a, rows, :] for a in range(3)]
            unit, same, along = pair_terms(target, source, wave, sign)
            projected = unit[0] * which[0] + unit[1] * which[1] + unit[2] * which[2]
            for part in range(2):
                scaled = along[part] * projected
                for a in range(3):
                    value = scaled * unit[a] + same[part] * which[a]
                    start = part * UNKNOWNS + a * HALF + chunk * CHUNK
                    far_k[number * 2 + half, start : start + CHUNK, :] = value.astype(jnp.bfloat16)

    def eval_near_others(wave, sign):
        def go(index, carry):
            near_eval(lax.div(index, 2), lax.rem(index, 2), wave, sign)
            return carry

        lax.fori_loop(2, 6, go, 0)

    def eval_far(start, stop, wave, sign):
        def go(index, carry):
            far_eval(lax.div(index, 2), lax.rem(index, 2), wave, sign)
            return carry

        lax.fori_loop(2 * start, 2 * stop, go, 0)

    def multiply_own(phase):
        near_wait(*raw_set[phase], 5 - my_half)
        fields = jnp.concatenate([raw_all[phase][4], raw_all[phase][5]], axis=1)
        acc_ref[...] = dot_nt(fields, near_k[0])

    def multiply_near(phase):
        def go(place, carry):
            slot = near_place(place) * 2
            fields = jnp.concatenate([raw_all[phase][slot], raw_all[phase][slot + 1]], axis=1)
            acc_ref[...] += dot_nt(fields, near_k[place])
            return carry

        lax.fori_loop(1, 3, go, 0)

    def multiply_far(phase):
        def go(number, carry):
            slot = far_tile(number) * 2
            charges = jnp.concatenate([chg_all[phase][slot], chg_all[phase][slot + 1]], axis=1)
            columns = jnp.concatenate([far_k[number * 2], far_k[number * 2 + 1]], axis=1)
            acc_ref[...] += dot_nt(charges, columns)
            return carry

        lax.fori_loop(0, tiles - 3, go, 0)

    def combined():
        real = acc_ref[:ANGLES, :UNKNOWNS] - acc_ref[ANGLES:, UNKNOWNS:]
        imag = acc_ref[:ANGLES, UNKNOWNS:] + acc_ref[ANGLES:, :UNKNOWNS]
        return real, imag

    loads = [
        pltpu.make_async_copy(src, dst, load_sem.at[number])
        for number, (src, dst) in enumerate(
            [
                (pos_in, pos_all.at[own_slot]),
                (fields_in, raw_all[0].at[own_slot]),
                (vf_in, vf_ref),
                (skel_in, skel_ref),
                (chi_in, chi_ref),
                (incident_in, incident_ref),
                (vh_in, vh_ref),
            ]
        )
    ]
    for load in loads:
        load.start()
    loads[0].wait()
    for a in range(3):
        target_ref[a] = jnp.broadcast_to(pos_all[own_slot, a], (HALF, HALF)).T
    near_eval(0, my_half, fund_wave, 1.0, True)
    loads[1].wait()
    loads[2].wait()
    loads[3].wait()
    pl.semaphore_wait(barrier, tiles)
    partner_send(*pos_set)
    near_sends(*pos_set)
    near_sends(*raw_set[0])
    partial(0, raw_all[0][own_slot], vf_ref)
    partner_send(*raw_set[0])

    near_wait(*pos_set, 5 - my_half)
    skeleton = skel_ref[...]
    component = jnp.where(skeleton >= 2 * POINTS, 2, jnp.where(skeleton >= POINTS, 1, 0))
    point = skeleton - component * POINTS
    lines = lax.broadcasted_iota(jnp.int32, (HALF, HALF), 0)
    masks = [lines + HALF * h == point for h in range(2)]
    packet = []
    for a in range(3):
        own_column = target_ref[a]
        other_column = jnp.broadcast_to(pos_all[5 - my_half, a], (HALF, HALF)).T
        columns = [
            jnp.where(my_half == 0, own_column, other_column),
            jnp.where(my_half == 0, other_column, own_column),
        ]
        picked = jnp.where(masks[0], columns[0], jnp.where(masks[1], columns[1], 0.0))
        packet.append(jnp.sum(picked, axis=0, keepdims=True))
    for a in range(3):
        packet.append((component == a).astype(jnp.float32))
    packet.append(jnp.zeros((2, HALF), jnp.float32))
    skel_all[me] = jnp.concatenate(packet, axis=0)
    far_sends(*skel_set)
    send_charges(0)

    near_forward(*pos_set)
    near_eval(0, 1 - my_half, fund_wave, 1.0, True)
    multiply_own(0)
    far_forward(*skel_set)
    near_arrive(*pos_set)
    eval_near_others(fund_wave, 1.0)
    near_forward(*raw_set[0])
    far_arrive(*skel_set)
    split = (tiles - 3) // 2
    eval_far(0, split, fund_wave, 1.0)
    far_forward(*chg_set[0])
    eval_far(split, tiles - 3, fund_wave, 1.0)
    near_arrive(*raw_set[0])
    multiply_near(0)
    far_arrive(*chg_set[0])
    multiply_far(0)

    loads[4].wait()
    loads[5].wait()
    loads[6].wait()
    real, imag = combined()
    real = incident_ref[:ANGLES, :].astype(jnp.float32) + real
    imag = incident_ref[ANGLES:, :].astype(jnp.float32) + imag
    fund_ref[:ANGLES, :] = real
    fund_ref[ANGLES:, :] = imag
    weights = jnp.concatenate([chi_ref[...]] * 3, axis=1)
    source = jnp.concatenate(
        [weights * (real * real - imag * imag), weights * 2.0 * real * imag], axis=0
    ).astype(jnp.bfloat16)

    raw_all[1][own_slot] = source
    near_sends(*raw_set[1])
    partial(1, source, vh_ref)
    partner_send(*raw_set[1])
    near_eval(0, my_half, harm_wave, -1.0, True)
    send_charges(1)
    near_eval(0, 1 - my_half, harm_wave, -1.0, True)
    multiply_own(1)
    eval_near_others(harm_wave, -1.0)
    near_forward(*raw_set[1])
    eval_far(0, split, harm_wave, -1.0)
    far_forward(*chg_set[1])
    eval_far(split, tiles - 3, harm_wave, -1.0)
    near_arrive(*raw_set[1])
    multiply_near(1)
    far_arrive(*chg_set[1])
    multiply_far(1)
    real, imag = combined()
    adj_ref[:ANGLES, :] = real
    adj_ref[ANGLES:, :] = imag

    near_sent(*pos_set)
    far_sent(*skel_set)
    for phase in range(2):
        part_copy(phase).wait_send()
        near_sent(*raw_set[phase])
        far_sent(*chg_set[phase])


def solution(mesh):
    slabs = mesh.shape["tiles"]
    tiles = slabs // 2
    bf16, f32 = jnp.bfloat16, jnp.float32
    dma = pltpu.SemaphoreType.DMA
    hbm = pl.BlockSpec(memory_space=pltpu.HBM)
    vmem = pl.BlockSpec(memory_space=pltpu.VMEM)

    def on_device(dipoles, incident, positions, chi, skeletons, near, vf, vh):
        fields = dipoles.reshape(ROWS, UNKNOWNS)
        out = jax.ShapeDtypeStruct((ROWS, UNKNOWNS), f32)
        fund, adj = pl.pallas_call(
            lambda *refs: body(slabs, *refs),
            out_shape=(out, out),
            in_specs=[hbm] * 5 + [pl.BlockSpec(memory_space=pltpu.SMEM)] + [hbm] * 2,
            out_specs=(vmem, vmem),
            scratch_shapes=[
                pltpu.VMEM((ROWS, UNKNOWNS), bf16),
                pltpu.VMEM((1, HALF), f32),
                pltpu.VMEM((1, HALF), jnp.int32),
                pltpu.VMEM((SKELETONS, UNKNOWNS), bf16),
                pltpu.VMEM((SKELETONS, UNKNOWNS), bf16),
                pltpu.VMEM((3, HALF, HALF), f32),
                pltpu.VMEM((10, 3, 1, HALF), f32),
                pltpu.VMEM((slabs, 8, HALF), f32),
                pltpu.VMEM((10, ROWS, UNKNOWNS), bf16),
                pltpu.VMEM((10, ROWS, UNKNOWNS), bf16),
                pltpu.VMEM((slabs, ROWS, HALF), bf16),
                pltpu.VMEM((slabs, ROWS, HALF), bf16),
                pltpu.VMEM((2, 2, ROWS, HALF), f32),
                pltpu.VMEM((2, ROWS, HALF), f32),
                pltpu.VMEM((3, 2 * UNKNOWNS, 2 * UNKNOWNS), bf16),
                pltpu.VMEM((2 * (tiles - 3), 2 * UNKNOWNS, HALF), bf16),
                pltpu.VMEM((ROWS, 2 * UNKNOWNS), f32),
                dma((9,)),
                dma((10,)),
                dma((slabs,)),
                dma((slabs,)),
                dma((2, 9)),
                dma((2, 10)),
                dma((2, slabs)),
                dma((2, slabs)),
                dma((2,)),
                dma((2,)),
                dma((7,)),
            ],
            compiler_params=pltpu.CompilerParams(
                collective_id=0, has_side_effects=True, vmem_limit_bytes=VMEM
            ),
            name="images",
        )(
            fields,
            incident.reshape(ROWS, UNKNOWNS),
            jnp.transpose(positions, (1, 0, 2)),
            chi,
            skeletons,
            near,
            vf[0],
            vh[0],
        )
        shape = (1, 2, ANGLES, UNKNOWNS)
        return fund.reshape(shape), adj.reshape(shape)

    row = ("groups", "tiles")
    in_specs = (
        P(row, None, None, None),
        P(row, None, None, None),
        P(row, None, None),
        P(row, None),
        P(row, None),
        P(row, None),
        P(row, None, None),
        P(row, None, None),
    )
    out_specs = (P(row, None, None, None), P(row, None, None, None))
    return jax.shard_map(
        on_device, mesh=mesh, in_specs=in_specs, out_specs=out_specs, check_vma=False
    )
```
